512 devices in a mesh: seq: 32 (over x, y), exp: 16 (over z, core).
Axes of the slice: x: 4, y: 8, z: 8, core: 2. Of those that a mesh axis runs over, the one named last changes fastest.
Arguments:
- conv_out: bfloat16 [4096, 8192], P('seq', 'exp'), may hold values from -6 to 6
- gate_z: bfloat16 [4096, 8192], P('seq', 'exp'), may hold values from -6 to 6
- delta_raw: bfloat16 [4096, 8192], P('seq', 'exp'), may hold values from -4 to 4
- decay_rate: float32 [8192, 16], P('exp'), may hold values from 0.0001 to 0.08
- b_proj: float32 [4096, 16], P('seq'), may hold values from -6 to 6
- c_proj: float32 [4096, 16], P('seq'), may hold values from -1.5 to 1.5
- skip_gain: float32 [8192], P('exp'), may hold values from 0.1 to 1.9
- out_weight: bfloat16 [8192, 4096], P('exp', 'seq'), may hold values from -0.0625 to 0.0625
- stream: bfloat16 [4096, 4096], P(('seq', 'exp')), may hold values from -6 to 6
- norm_gain: float32 [4096], replicated, may hold values from 0.1 to 1.9
- expert_ids: int32 [4096, 2], P(('seq', 'exp')), may hold values from 0 to 15, all different within a row; in each aligned block of 8 rows (0 to 7, 8 to 15, ...) at most 2 rows name the same one
- gate_weights: bfloat16 [4096, 2], P(('seq', 'exp')), may hold values from 0.099609375 to 0.8984375
- w_gate: bfloat16 [16, 7168, 4096], P('exp', 'seq'), may hold values from -0.09375 to 0.09375
- w_up: bfloat16 [16, 7168, 4096], P('exp', 'seq'), may hold values from -0.09375 to 0.09375
Outputs:
- expert_hidden: bfloat16 [16, 7168, 1024], P('exp', 'seq')
The draws below stay inside these ranges and needn't reach their ends.
Inputs may be any that keep to these rules, and one draw needn't show every extreme that they name: `expert_ids`: the two ids of a token differ; among the 8 tokens of one aligned block no expert is named more than 2 times, a bound that some block reaches.
All inputs are finite; a program needn't handle non-finite values.
Results may differ from the reference program's by a relative error of at most 0.0071.
Values may be sent and summed in bfloat16 or wider, within the bound.
No kernel may reach another device: no remote copies, remote signals or barrier semaphores. Data moves between devices by JAX's collectives and lax.ppermute only.
A program may use at most 64 MiB of HBM per device.

```python
import math
import jax
import jax.numpy as jnp
import numpy as np
from jax import lax

D = 4096
INNER = 8192
STATES = 16
FFW = 7168
EXPERTS = 16
TOKENS = 4096
TOK_DEV = 8
MOST = 2
SLOTS = 1024


def level_of(own_key, extent, shards, least, top_value):
    def one(dim, parts):
        heights = jax.random.uniform(jax.random.fold_in(jax.random.fold_in(own_key, 6), dim), (parts,), jnp.float32, least / len(shards), top_value / len(shards))
        return jnp.repeat(jnp.exp(heights), extent[dim] // parts).reshape((-1,) + (1,) * (len(extent) - dim - 1))

    gain = one(*shards[0])
    for cut in shards[1:]:
        gain = gain * one(*cut)
    return gain


def routed_block(own_key, own, number, rows, amount, top, limit, slope):
    order = jax.random.permutation(own_key, amount)
    packed, usual = shares(amount, rows * top, limit, slope, True), shares(amount, rows * top, limit, slope, False)
    places = jnp.arange(amount)

    def named(sizes, rotation):
        used = int((sizes > 0).sum())
        fixed = max(1, used // 4)
        passed = fixed + (places - fixed + rotation * (used - fixed)) % max(1, amount - fixed)
        return jnp.zeros((amount,), jnp.int32).at[order[jnp.where(places < fixed, places, passed)]].set(jnp.asarray(sizes, jnp.int32))

    sizes = jnp.where(number % 4 == 0, named(packed, number // 4), named(usual, number - number // 4 - 1))
    mixed = jax.random.permutation(jax.random.fold_in(own, 3), amount)
    source_of, sink = mixed[0:amount // 2 * 2:2], mixed[1:amount // 2 * 2:2]
    room = jnp.minimum(sizes[source_of] - 1, limit - sizes[sink]) // 2
    room = jnp.where((source_of == order[0]) | (sink == order[0]) | (sizes[sink] == 0), 0, jnp.maximum(room, 0))
    passed = jax.random.randint(jax.random.fold_in(own, 4), (amount // 2,), 0, 1 << 20) % (room + 1)
    sizes = sizes.at[source_of].add(-passed).at[sink].add(passed)
    labels = jnp.searchsorted(jnp.cumsum(sizes), jnp.arange(rows * top), side="right").astype(jnp.int32)
    table = labels.reshape(top, rows).T
    table = table[jax.random.permutation(jax.random.fold_in(own, 1), rows)]
    rotation = jax.random.randint(jax.random.fold_in(own, 2), (rows, 1), 0, top)
    return jnp.take_along_axis(table, (jnp.arange(top)[None, :] + rotation) % top, axis=1)


def shares(count, total, reach, slope, full):
    loads = [(1 << 20) // math.isqrt(grade ** slope) + 1 for grade in range(1, count + 1)]
    largest = reach if full else min(reach, max(-(-total // count), total * loads[0] // sum(loads)))
    least = 1 if total - largest >= count - 1 else 0
    given, surplus = [largest] + [least] * (count - 1), total - largest - least * (count - 1)
    while surplus > 0:
        free = [i for i in range(1, count) if given[i] < largest] or [i for i in range(1, count) if given[i] < reach]
        pool, budget = sum([loads[i] for i in free]), surplus
        for i in free:
            more = min(reach - given[i], max(1, budget * loads[i] // pool), surplus)
            given[i] = given[i] + more
            surplus = surplus - more
    return np.array(given)


def bell_draw(rng, shape, deviation, most, pieces=(), held_as=jnp.bfloat16):
    gain = level_of(rng, shape, pieces, -0.22, 0.18) if pieces else 1.0
    array = jax.random.normal(rng, shape, jnp.float32) * deviation * gain
    return jnp.minimum(jnp.maximum(array, -most), most).astype(held_as)


def setup_inputs(seed: int = 0) -> dict:
    keys = jax.random.split(jax.random.key(seed), 15)
    conv_out = bell_draw(keys[0], (TOKENS, INNER), 1.0, 6.0, ((0, 32), (1, 16)))
    gate_z = bell_draw(keys[1], (TOKENS, INNER), 1.0, 6.0, ((0, 32), (1, 16)))
    delta_raw = bell_draw(keys[2], (TOKENS, INNER), 1.0, 4.0, ((0, 32), (1, 16)))
    decay_rate = jnp.clip(jnp.exp(math.log(0.08) - 6.684612 * jax.random.uniform(keys[3], (INNER, STATES), jnp.float32) ** level_of(keys[3], (INNER, STATES), ((0, 16),), -0.2, 0.2)), 0.0001, 0.08)
    b_proj = bell_draw(keys[4], (TOKENS, STATES), 1.0, 6.0, ((0, 32),), jnp.float32)
    c_proj = bell_draw(keys[5], (TOKENS, STATES), 0.25, 1.5, ((0, 32),), jnp.float32)
    skip_gain = jnp.clip(1.0 + 0.18 * jax.random.normal(keys[6], (INNER,), jnp.float32), 0.1, 1.9)
    out_weight = bell_draw(keys[7], (INNER, D), INNER ** -0.5, 0.0625, ((0, 16), (1, 32)))
    stream = bell_draw(keys[8], (TOKENS, D), 1.0, 6.0, ((0, 512),))
    norm_gain = jnp.clip(1.0 + 0.18 * jax.random.normal(keys[9], (D,), jnp.float32), 0.1, 1.9)
    expert_ids_keys = jax.random.split(jax.random.fold_in(keys[10], 1), TOKENS // TOK_DEV)
    expert_ids_turns = jax.random.permutation(jax.random.fold_in(keys[10], 3), TOKENS // TOK_DEV)
    expert_ids = jax.vmap(lambda own, number: routed_block(jax.random.fold_in(keys[10], 2), own, number, TOK_DEV, EXPERTS, 2, MOST, 1))(expert_ids_keys, expert_ids_turns).reshape((TOKENS, 2))
    gate_weights = jnp.clip(0.099609375 + 0.7988281 * jax.random.uniform(keys[11], (TOKENS, 2), jnp.float32) ** level_of(keys[11], (TOKENS, 2), ((0, 512),), -0.2, 0.2), 0.099609375, 0.8984375).astype(jnp.bfloat16)
    w_gate = bell_draw(keys[12], (EXPERTS, FFW, D), D ** -0.5, 0.09375, ((0, 16), (1, 32)))
    w_up = bell_draw(keys[13], (EXPERTS, FFW, D), D ** -0.5, 0.09375, ((0, 16), (1, 32)))
    return dict(conv_out=conv_out, gate_z=gate_z, delta_raw=delta_raw, decay_rate=decay_rate, b_proj=b_proj, c_proj=c_proj, skip_gain=skip_gain, out_weight=out_weight, stream=stream, norm_gain=norm_gain, expert_ids=expert_ids, gate_weights=gate_weights, w_gate=w_gate, w_up=w_up)


def reference(conv_out, gate_z, delta_raw, decay_rate, b_proj, c_proj, skip_gain, out_weight, stream, norm_gain, expert_ids, gate_weights, w_gate, w_up):
    inputs = conv_out.astype(jnp.float32)
    steps = jax.nn.softplus(delta_raw.astype(jnp.float32))

    def advance(state, item):
        xt, dtt, bt, ct = item
        state = jnp.exp(dtt[:, None] * -decay_rate) * state + (dtt * xt)[:, None] * bt[None, :]
        return (state, lax.optimization_barrier(jnp.sum(state * ct[None, :], axis=1)))
    start = jnp.zeros((INNER, STATES), jnp.float32)
    _, ssm = lax.scan(advance, start, (inputs, steps, b_proj, c_proj))
    gated = ((ssm + skip_gain[None, :] * inputs) * jax.nn.silu(gate_z.astype(jnp.float32))).astype(jnp.bfloat16)
    mixed = jnp.dot(gated, out_weight, preferred_element_type=jnp.float32)
    resid = stream.astype(jnp.float32) + mixed
    scale = lax.rsqrt(lax.optimization_barrier(jnp.mean(resid * resid, axis=1, keepdims=True)) + 1e-05)
    normed = (resid * scale * norm_gain[None, :]).astype(jnp.bfloat16)
    blocks = TOKENS // TOK_DEV
    onehot = (expert_ids[:, :, None] == jnp.arange(EXPERTS, dtype=jnp.int32)[None, None, :]).astype(jnp.int32)
    flat = onehot.reshape(blocks, TOK_DEV * 2, EXPERTS)
    before = jnp.cumsum(flat, axis=1) - flat
    position = lax.optimization_barrier(jnp.sum(before * flat, axis=2)).reshape(TOKENS, 2)
    block_id = (jnp.arange(TOKENS, dtype=jnp.int32) // TOK_DEV)[:, None]
    slot = (block_id * MOST + position).astype(jnp.int32)
    rows = jnp.broadcast_to(normed[:, None, :], (TOKENS, 2, D))
    slot_rows = jnp.zeros((EXPERTS, SLOTS, D), jnp.bfloat16).at[expert_ids, slot].set(rows)
    slot_gate = jnp.zeros((EXPERTS, SLOTS), jnp.bfloat16).at[expert_ids, slot].set(gate_weights)

    def expert(item):
        rows_e, gate_e, wg, wu = item
        dims = (((1,), (1,)), ((), ()))
        hidden = lax.dot_general(wg, rows_e, dims, preferred_element_type=jnp.float32)
        upward = lax.dot_general(wu, rows_e, dims, preferred_element_type=jnp.float32)
        return (jax.nn.silu(hidden) * upward * gate_e.astype(jnp.float32)[None, :]).astype(jnp.bfloat16)
    return lax.map(expert, (slot_rows, slot_gate, w_gate, w_up))
```

```python
import jax
import jax.numpy as jnp
import numpy as np
from jax import lax
from jax.experimental import pallas as pl
from jax.experimental.pallas import tpu as pltpu
from jax.sharding import Mesh
from jax.sharding import PartitionSpec as P

NX, NY = 4, 8
SEQ = ("x", "y")
EXP = ("z", "c")
LOG2E = 1.4426950408889634
SPAN = 16
PAD = 128
TURN = 256
MIB = 1024 * 1024


def softplus(v):
    return jnp.maximum(v, 0.0) + jnp.log1p(jnp.exp(-jnp.abs(v)))


def last_kernel(x_ref, d_ref, rate_ref, b_ref, part_ref):
    rate = rate_ref[...]
    states, width = rate.shape

    def some(i, carry):
        state, total = carry
        rows = pl.ds(pl.multiple_of(i * SPAN, SPAN), SPAN)
        dt = softplus(d_ref[rows, :].astype(jnp.float32))
        u = dt * x_ref[rows, :].astype(jnp.float32)
        b = b_ref[i]
        for t in range(SPAN):
            step = dt[t : t + 1, :]
            state = jnp.exp2(rate * step) * state + b[:, t : t + 1] * u[t : t + 1, :]
            total = total + step
        return state, total

    start = (jnp.zeros((states, width), jnp.float32), jnp.zeros((1, width), jnp.float32))
    state, total = lax.fori_loop(0, x_ref.shape[0] // SPAN, some, start)
    part_ref[:states, :] = state
    part_ref[states:, :] = jnp.broadcast_to(total, (8, width))


def row_kernel(y_ref, parts_ref, rate_ref, near_ref, row_ref):
    rate = rate_ref[...]
    states, width = rate.shape
    y = y_ref[0]
    state, total = jnp.zeros((states, width), jnp.float32), jnp.zeros((8, width), jnp.float32)
    near, near_total = state, total
    for k in range(parts_ref.shape[0]):
        sums = parts_ref[k, states:, :]
        decay = jnp.exp2(rate * sums[0:1])
        state = decay * state + parts_ref[k, :states, :]
        total = total + sums
        near = jnp.where(k + 1 == y, state, near)
        near_total = jnp.where(k + 1 == y, total, near_total)
    near_ref[:states, :] = near
    near_ref[states:, :] = near_total
    row_ref[:states, :] = state
    row_ref[states:, :] = total


def gated_kernel(place_ref, x_ref, d_ref, z_ref, rate_ref, b_ref, c_ref, skip_ref, near_ref, rows_ref, out_ref):
    rate = rate_ref[...]
    states, width = rate.shape
    place = lax.broadcasted_iota(jnp.int32, (SPAN, width), 0)
    start = jnp.zeros((states, width), jnp.float32)
    for k in range(rows_ref.shape[0] - 1):
        later = jnp.exp2(rate * rows_ref[k, states : states + 1, :]) * start + rows_ref[k, :states, :]
        start = jnp.where(k < place_ref[0], later, start)
    start = jnp.exp2(rate * near_ref[states : states + 1, :]) * start + near_ref[:states, :]

    def some(i, state):
        rows = pl.ds(pl.multiple_of(i * SPAN, SPAN), SPAN)
        dt = softplus(d_ref[rows, :].astype(jnp.float32))
        x = x_ref[rows, :].astype(jnp.float32)
        u = dt * x
        b, c = b_ref[i], c_ref[i]
        ssm = jnp.zeros((SPAN, width), jnp.float32)
        for t in range(SPAN):
            step = dt[t : t + 1, :]
            state = jnp.exp2(rate * step) * state + b[:, t : t + 1] * u[t : t + 1, :]
            row = jnp.sum(state * c[:, t : t + 1], axis=0, keepdims=True)
            ssm = jnp.where(place == t, row, ssm)
        z = z_ref[rows, :].astype(jnp.float32)
        gate = z / (1.0 + jnp.exp(-z))
        out_ref[rows, :] = ((ssm + skip_ref[...] * x) * gate).astype(jnp.bfloat16)
        return state

    lax.fori_loop(0, x_ref.shape[0] // SPAN, some, start)


def project_kernel(core_ref, g_ref, w_ref, own_ref, other_ref):
    n_x, zs, tok, _ = own_ref.shape
    n_y, _, wide = w_ref.shape
    g = g_ref[...].reshape(n_x * zs * 2 * tok, g_ref.shape[2])
    first = core_ref[0] == 0
    for y in range(0, n_y, 2):
        w = jnp.concatenate([w_ref[y], w_ref[y + 1]], axis=1)
        p = jnp.dot(g, w, preferred_element_type=jnp.float32)
        p = p.reshape(n_x, zs, 2, tok, 2 * wide)
        a, b = p[:, :, 0], p[:, :, 1]
        at = y * wide
        own_ref[:, :, :, at : at + 2 * wide] = jnp.where(first, a, b)
        other_ref[:, :, :, at : at + 2 * wide] = jnp.where(first, b, a).astype(jnp.bfloat16)


def slots_kernel(got_ref, stream_ref, gain_ref, sel_ref, gate_ref, out_ref):
    zs = got_ref.shape[0] // NX
    blocks = []
    for x in range(NX):
        block = got_ref[x * zs].astype(jnp.float32)
        for z in range(1, zs):
            block = block + got_ref[x * zs + z].astype(jnp.float32)
        blocks.append(block)
    resid = stream_ref[...].astype(jnp.float32) + jnp.concatenate(blocks, axis=1)
    mean = jnp.mean(resid * resid, axis=1, keepdims=True)
    normed = (resid * lax.rsqrt(mean + 1e-05) * gain_ref[...]).astype(jnp.bfloat16).astype(jnp.float32)
    sel = sel_ref[...]
    rows = sel[:, 0:1] * normed[0:1, :]
    for t in range(1, normed.shape[0]):
        rows = rows + sel[:, t : t + 1] * normed[t : t + 1, :]
    width = normed.shape[1]
    out_ref[:, :width] = rows.astype(jnp.bfloat16)
    out_ref[:, width:] = gate_ref[...]


def turn_kernel(wg_ref, wu_ref, out_ref):
    units = wg_ref.shape[0]
    block = out_ref.shape[1] // 2

    def some(i, _):
        at = pl.ds(pl.multiple_of(i * TURN, TURN), TURN)
        for k, ref in enumerate((wg_ref, wu_ref)):
            w = ref[:, at].astype(jnp.float32)
            if block > units:
                w = jnp.concatenate([w, jnp.zeros((block - units, TURN), jnp.float32)], axis=0)
            out_ref[at, k * block : (k + 1) * block] = w.T.astype(jnp.bfloat16)
        return 0

    lax.fori_loop(0, wg_ref.shape[1] // TURN, some, 0)


def experts_kernel(place_ref, a0, a1, a20, a21, a3, b0, b1, b2, b3, b40, b41, b5, b6, b7, w_ref, out_ref, b):
    my_x, my_y = place_ref[0], place_ref[1]
    units = out_ref.shape[0]
    block = w_ref.shape[1] // 2
    slots = b0.shape[1]
    wide = a0.shape[1]
    rest = w_ref.shape[0] - wide
    group = NY * slots
    for dx in range(NX):
        x = lax.rem(my_x - dx + NX, NX)
        for dy, ref in enumerate((b0, b1, b2, b3, None, b5, b6, b7)):
            y = lax.rem(my_y - dy + NY, NY)
            at = pl.ds(pl.multiple_of(y * slots, slots), slots)
            if ref is None:

                @pl.when(x < NX // 2)
                def _():
                    b[at, :] = b40[x]

                @pl.when(x >= NX // 2)
                def _():
                    b[at, :] = b41[x - NX // 2]

            else:
                b[at, :] = ref[x]
        if dx == 2:
            first = jnp.concatenate([a20[...], a21[...]], axis=0)
        else:
            first = (a0, a1, None, a3)[dx][...]
        p = jnp.dot(first, w_ref[:wide, :], preferred_element_type=jnp.float32)
        p = p + jnp.dot(b[:, :rest], w_ref[wide:, :], preferred_element_type=jnp.float32)
        gate = b[:, rest:].astype(jnp.float32)[:, 0:1]
        hidden, upward = p[:, :block], p[:, block:]
        value = hidden / (1.0 + jnp.exp(-hidden)) * upward * gate
        to = pl.ds(pl.multiple_of(x * group, group), group)
        out_ref[:, to] = value.T[:units].astype(jnp.bfloat16)


def spread(a, axis, size):
    copies = jnp.broadcast_to(a[None], (size,) + a.shape)
    return lax.all_to_all(copies, axis, split_axis=0, concat_axis=0, tiled=True)


def ring(a, axis, size, hop):
    return lax.ppermute(a, axis, [(i, (i + hop) % size) for i in range(size)])


def everywhere(rows):
    slots, width = rows.shape
    wide = (width - PAD) // 2
    a, b = rows[:, :wide], rows[:, wide:]
    a0 = lax.all_gather(a, "y").reshape(NY * slots, wide)
    b0 = spread(b, "x", NX)
    s1, t1 = ring(b0, "y", NY, 1), ring(b0, "y", NY, -1)
    a0, s1, t1 = lax.optimization_barrier((a0, s1, t1))
    ap, am = ring(a0, "x", NX, 1), ring(a0, "x", NX, -1)
    s2, t2 = ring(s1, "y", NY, 1), ring(t1, "y", NY, -1)
    s3, t3 = ring(s2, "y", NY, 1), ring(t2, "y", NY, -1)
    s4, t4 = ring(s3[: NX // 2], "y", NY, 1), ring(t3[NX // 2 :], "y", NY, -1)
    half = NY * slots // 2
    ao0, ao1 = ring(ap[:half], "x", NX, 1), ring(am[half:], "x", NX, -1)
    return [a0, ap, ao0, ao1, am], [b0, s1, s2, s3, s4, t4, t3, t2, t1]


VMEM = pl.BlockSpec(memory_space=pltpu.VMEM)
SMEM = pl.BlockSpec(memory_space=pltpu.SMEM)


def body(
    conv_out,
    gate_z,
    delta_raw,
    decay_rate,
    b_proj,
    c_proj,
    skip_gain,
    out_weight,
    stream,
    norm_gain,
    expert_ids,
    gate_weights,
    w_gate,
    w_up,
):
    tokens, width = conv_out.shape
    states = decay_rate.shape[1]
    tok_rows, features = stream.shape
    n_z = lax.axis_size("z")
    n_experts = n_z * 2
    small = pltpu.CompilerParams(vmem_limit_bytes=12 * MIB)

    columns = lax.all_gather(out_weight, "y")
    place = jnp.stack([lax.axis_index("x"), lax.axis_index("y")]).astype(jnp.int32)

    rate = decay_rate.T * -LOG2E
    spans = tokens // SPAN
    b3 = b_proj.reshape(spans, SPAN, states).transpose(0, 2, 1)
    c3 = c_proj.reshape(spans, SPAN, states).transpose(0, 2, 1)
    work = tokens * width * states
    part = pl.pallas_call(
        last_kernel,
        out_shape=jax.ShapeDtypeStruct((states + 8, width), jnp.float32),
        in_specs=[VMEM] * 4,
        out_specs=VMEM,
        compiler_params=small,
        cost_estimate=pl.CostEstimate(flops=4 * work, bytes_accessed=1 << 18, transcendentals=work),
    )(conv_out, delta_raw, rate, b3)
    part_shape = jax.ShapeDtypeStruct(part.shape, jnp.float32)
    near, row = pl.pallas_call(
        row_kernel,
        out_shape=[part_shape, part_shape],
        in_specs=[SMEM, VMEM, VMEM],
        out_specs=[VMEM, VMEM],
        compiler_params=small,
        cost_estimate=pl.CostEstimate(flops=1 << 18, bytes_accessed=1 << 19, transcendentals=1 << 16),
    )(place[1:], spread(part, "y", NY), rate)
    rows_before = spread(row, "x", NX)
    gated = pl.pallas_call(
        gated_kernel,
        out_shape=jax.ShapeDtypeStruct((tokens, width), jnp.bfloat16),
        in_specs=[SMEM] + [VMEM] * 9,
        out_specs=VMEM,
        compiler_params=small,
        cost_estimate=pl.CostEstimate(flops=6 * work, bytes_accessed=1 << 19, transcendentals=work),
    )(place[:1], conv_out, delta_raw, gate_z, rate, b3, c3, skip_gain[None, :], near, rows_before)

    core = lax.axis_index("c").astype(jnp.int32).reshape(1)
    shape = (NX, n_z, tok_rows, features // NX)
    own, other = pl.pallas_call(
        project_kernel,
        out_shape=[jax.ShapeDtypeStruct(shape, jnp.float32), jax.ShapeDtypeStruct(shape, jnp.bfloat16)],
        in_specs=[SMEM, VMEM, VMEM],
        out_specs=[VMEM, VMEM],
        compiler_params=small,
        cost_estimate=pl.CostEstimate(
            flops=2 * tokens * width * features, bytes_accessed=width * features * 2, transcendentals=0
        ),
    )(core, spread(gated, "x", NX), columns)
    theirs = ring(other, "c", 2, 1)
    both = (own + theirs.astype(jnp.float32)).astype(jnp.bfloat16)
    both = both.reshape(NX * n_z, tok_rows, features // NX)
    both, wg, wu = lax.optimization_barrier((both, w_gate[0], w_up[0]))
    hidden_units = w_gate.shape[1]
    block = -(-hidden_units // TURN) * TURN
    turned = pl.pallas_call(
        turn_kernel,
        out_shape=jax.ShapeDtypeStruct((features, 2 * block), jnp.bfloat16),
        in_specs=[VMEM] * 2,
        out_specs=VMEM,
        compiler_params=small,
        cost_estimate=pl.CostEstimate(flops=1 << 24, bytes_accessed=16 * MIB, transcendentals=0),
    )(wg, wu)
    got = lax.all_to_all(both, ("x", "z"), split_axis=0, concat_axis=0, tiled=True)

    most_slots = 4 * tok_rows // n_experts
    onehot = (
        expert_ids[:, :, None] == jnp.arange(n_experts, dtype=jnp.int32)[None, None, :]
    ).astype(jnp.int32)
    flat = onehot.reshape(tok_rows * 2, n_experts)
    before = jnp.cumsum(flat, axis=0) - flat
    position = jnp.sum(before * flat, axis=1).reshape(tok_rows, 2)
    matched = (
        position[:, :, None] == jnp.arange(most_slots, dtype=jnp.int32)[None, None, :]
    ).astype(jnp.float32)
    pairs = onehot.astype(jnp.float32)[:, :, :, None] * matched[:, :, None, :]
    slots = n_experts * most_slots
    sel = jnp.sum(pairs, axis=1).reshape(tok_rows, slots).T
    gate = jnp.sum(pairs * gate_weights.astype(jnp.float32)[:, :, None, None], axis=(0, 1)).reshape(slots, 1)
    gate = jnp.pad(gate, ((0, 0), (0, PAD - 1))).astype(jnp.bfloat16)

    rows = pl.pallas_call(
        slots_kernel,
        out_shape=jax.ShapeDtypeStruct((slots, features + PAD), jnp.bfloat16),
        in_specs=[VMEM] * 5,
        out_specs=VMEM,
        compiler_params=small,
        cost_estimate=pl.CostEstimate(flops=1 << 21, bytes_accessed=1 << 20, transcendentals=0),
    )(got, stream, norm_gain[None, :], sel, gate)
    rows = rows.reshape(n_experts, most_slots, features + PAD)
    rows = lax.all_to_all(rows, EXP, split_axis=0, concat_axis=0, tiled=True)
    a_parts, b_parts = everywhere(rows.reshape(slots, features + PAD))

    total = NX * NY * slots
    result = pl.pallas_call(
        experts_kernel,
        out_shape=jax.ShapeDtypeStruct((hidden_units, total), jnp.bfloat16),
        in_specs=[SMEM] + [VMEM] * 15,
        out_specs=VMEM,
        scratch_shapes=[pltpu.VMEM((NY * slots, features // 2 + PAD), jnp.bfloat16)],
        compiler_params=pltpu.CompilerParams(vmem_limit_bytes=28 * MIB),
        cost_estimate=pl.CostEstimate(
            flops=4 * hidden_units * total * features,
            bytes_accessed=total * features * 2,
            transcendentals=hidden_units * total,
        ),
    )(place, *a_parts, *b_parts, turned)
    return result[None]


def solution(mesh):
    n_z = mesh.shape["exp"] // 2
    fine = Mesh(np.asarray(mesh.devices).reshape(NX, NY, n_z, 2), ("x", "y", "z", "c"))
    in_specs = (
        P(SEQ, EXP),
        P(SEQ, EXP),
        P(SEQ, EXP),
        P(EXP, None),
        P(SEQ, None),
        P(SEQ, None),
        P(EXP),
        P(EXP, SEQ),
        P(SEQ + EXP, None),
        P(),
        P(SEQ + EXP, None),
        P(SEQ + EXP, None),
        P(EXP, SEQ, None),
        P(EXP, SEQ, None),
    )
    out_specs = P(EXP, SEQ, None)
    return jax.shard_map(body, mesh=fine, in_specs=in_specs, out_specs=out_specs, check_vma=False)
```

```python
import jax
import jax.numpy as jnp
import numpy as np
from jax import lax
from jax.experimental import pallas as pl
from jax.experimental.pallas import tpu as pltpu
from jax.sharding import Mesh
from jax.sharding import PartitionSpec as P

NX, NY = 4, 8
SEQ = ("x", "y")
EXP = ("z", "c")
LOG2E = 1.4426950408889634
SPAN = 16
PAD = 128
TURN = 256
MIB = 1024 * 1024


def softplus(v):
    return jnp.maximum(v, 0.0) + jnp.log1p(jnp.exp(-jnp.abs(v)))


def last_kernel(x_ref, d_ref, rate_ref, b_ref, part_ref):
    rate = rate_ref[...]
    states, width = rate.shape

    def some(i, carry):
        state, total = carry
        rows = pl.ds(pl.multiple_of(i * SPAN, SPAN), SPAN)
        dt = softplus(d_ref[rows, :].astype(jnp.float32))
        u = dt * x_ref[rows, :].astype(jnp.float32)
        b = b_ref[i]
        for t in range(SPAN):
            step = dt[t : t + 1, :]
            state = jnp.exp2(rate * step) * state + b[:, t : t + 1] * u[t : t + 1, :]
            total = total + step
        return state, total

    start = (jnp.zeros((states, width), jnp.float32), jnp.zeros((1, width), jnp.float32))
    state, total = lax.fori_loop(0, x_ref.shape[0] // SPAN, some, start)
    for k in range(part_ref.shape[0]):
        part_ref[k, :states, :] = state
        part_ref[k, states:, :] = jnp.broadcast_to(total, (8, width))


def row_kernel(y_ref, parts_ref, rate_ref, near_ref, row_ref):
    rate = rate_ref[...]
    states, width = rate.shape
    y = y_ref[0]
    state, total = jnp.zeros((states, width), jnp.float32), jnp.zeros((8, width), jnp.float32)
    near, near_total = state, total
    for k in range(parts_ref.shape[0]):
        sums = parts_ref[k, states:, :]
        decay = jnp.exp2(rate * sums[0:1])
        state = decay * state + parts_ref[k, :states, :]
        total = total + sums
        near = jnp.where(k + 1 == y, state, near)
        near_total = jnp.where(k + 1 == y, total, near_total)
    near_ref[:states, :] = near
    near_ref[states:, :] = near_total
    for k in range(row_ref.shape[0]):
        row_ref[k, :states, :] = state
        row_ref[k, states:, :] = total


def gated_kernel(place_ref, x_ref, d_ref, z_ref, rate_ref, b_ref, c_ref, skip_ref, near_ref, rows_ref, out_ref):
    rate = rate_ref[...]
    states, width = rate.shape
    place = lax.broadcasted_iota(jnp.int32, (SPAN, width), 0)
    start = jnp.zeros((states, width), jnp.float32)
    for k in range(rows_ref.shape[0] - 1):
        later = jnp.exp2(rate * rows_ref[k, states : states + 1, :]) * start + rows_ref[k, :states, :]
        start = jnp.where(k < place_ref[0], later, start)
    start = jnp.exp2(rate * near_ref[states : states + 1, :]) * start + near_ref[:states, :]

    def some(i, state):
        rows = pl.ds(pl.multiple_of(i * SPAN, SPAN), SPAN)
        dt = softplus(d_ref[rows, :].astype(jnp.float32))
        x = x_ref[rows, :].astype(jnp.float32)
        u = dt * x
        b, c = b_ref[i], c_ref[i]
        ssm = jnp.zeros((SPAN, width), jnp.float32)
        for t in range(SPAN):
            step = dt[t : t + 1, :]
            state = jnp.exp2(rate * step) * state + b[:, t : t + 1] * u[t : t + 1, :]
            row = jnp.sum(state * c[:, t : t + 1], axis=0, keepdims=True)
            ssm = jnp.where(place == t, row, ssm)
        z = z_ref[rows, :].astype(jnp.float32)
        gate = z / (1.0 + jnp.exp(-z))
        gated = ((ssm + skip_ref[...] * x) * gate).astype(jnp.bfloat16)
        for k in range(out_ref.shape[0]):
            out_ref[k, rows, :] = gated
        return state

    lax.fori_loop(0, x_ref.shape[0] // SPAN, some, start)


def project_kernel(core_ref, g_ref, w_ref, own_ref, other_ref):
    n_x, zs, tok, _ = own_ref.shape
    n_y, _, wide = w_ref.shape
    g = g_ref[...].reshape(n_x * zs * 2 * tok, g_ref.shape[2])
    first = core_ref[0] == 0
    for y in range(0, n_y, 2):
        w = jnp.concatenate([w_ref[y], w_ref[y + 1]], axis=1)
        p = jnp.dot(g, w, preferred_element_type=jnp.float32)
        p = p.reshape(n_x, zs, 2, tok, 2 * wide)
        a, b = p[:, :, 0], p[:, :, 1]
        at = y * wide
        own_ref[:, :, :, at : at + 2 * wide] = jnp.where(first, a, b)
        other_ref[:, :, :, at : at + 2 * wide] = jnp.where(first, b, a).astype(jnp.bfloat16)


def slots_kernel(got_ref, stream_ref, gain_ref, sel_ref, gate_ref, a_ref, b_ref):
    zs = got_ref.shape[0] // NX
    blocks = []
    for x in range(NX):
        block = got_ref[x * zs].astype(jnp.float32)
        for z in range(1, zs):
            block = block + got_ref[x * zs + z].astype(jnp.float32)
        blocks.append(block)
    resid = stream_ref[...].astype(jnp.float32) + jnp.concatenate(blocks, axis=1)
    mean = jnp.mean(resid * resid, axis=1, keepdims=True)
    normed = (resid * lax.rsqrt(mean + 1e-05) * gain_ref[...]).astype(jnp.bfloat16).astype(jnp.float32)
    sel = sel_ref[...]
    rows = sel[:, 0:1] * normed[0:1, :]
    for t in range(1, normed.shape[0]):
        rows = rows + sel[:, t : t + 1] * normed[t : t + 1, :]
    wide = b_ref.shape[1]
    a_ref[:, :wide] = rows[:, :wide].astype(jnp.bfloat16)
    a_ref[:, wide:] = gate_ref[...]
    b_ref[...] = rows[:, wide:].astype(jnp.bfloat16)


def turn_kernel(wg_ref, wu_ref, out_ref):
    units = wg_ref.shape[0]
    block = out_ref.shape[1] // 2

    def some(i, _):
        at = pl.ds(pl.multiple_of(i * TURN, TURN), TURN)
        for k, ref in enumerate((wg_ref, wu_ref)):
            w = ref[:, at].astype(jnp.float32)
            if block > units:
                w = jnp.concatenate([w, jnp.zeros((block - units, TURN), jnp.float32)], axis=0)
            out_ref[at, k * block : (k + 1) * block] = w.T.astype(jnp.bfloat16)
        return 0

    lax.fori_loop(0, wg_ref.shape[1] // TURN, some, 0)


def experts_kernel(place_ref, a0, a1, a20, a21, a3, b0, b1, b2, b3, b40, b41, b5, b6, b7, w_ref, out_ref, b):
    my_x, my_y = place_ref[0], place_ref[1]
    units = out_ref.shape[0]
    block = w_ref.shape[1] // 2
    slots = b0.shape[1]
    wide = a0.shape[1] - PAD
    group = NY * slots
    for dx in range(NX):
        x = lax.rem(my_x - dx + NX, NX)
        for dy, ref in enumerate((b0, b1, b2, b3, None, b5, b6, b7)):
            y = lax.rem(my_y - dy + NY, NY)
            at = pl.ds(pl.multiple_of(y * slots, slots), slots)
            if ref is None:

                @pl.when(x < NX // 2)
                def _():
                    b[at, :] = b40[x]

                @pl.when(x >= NX // 2)
                def _():
                    b[at, :] = b41[x - NX // 2]

            else:
                b[at, :] = ref[x]
        if dx == 2:
            first = jnp.concatenate([a20[...], a21[...]], axis=0)
        else:
            first = (a0, a1, None, a3)[dx][...]
        p = jnp.dot(first[:, :wide], w_ref[:wide, :], preferred_element_type=jnp.float32)
        p = p + jnp.dot(b[...], w_ref[wide:, :], preferred_element_type=jnp.float32)
        gate = first[:, wide:].astype(jnp.float32)[:, 0:1]
        hidden, upward = p[:, :block], p[:, block:]
        value = hidden / (1.0 + jnp.exp(-hidden)) * upward * gate
        to = pl.ds(pl.multiple_of(x * group, group), group)
        out_ref[:, to] = value.T[:units].astype(jnp.bfloat16)


def spread(copies, axis):
    return lax.all_to_all(copies, axis, split_axis=0, concat_axis=0, tiled=True)


def ring(a, axis, size, hop):
    return lax.ppermute(a, axis, [(i, (i + hop) % size) for i in range(size)])


def dispatched(rows, n_experts):
    slots, width = rows.shape
    rows = rows.reshape(n_experts, slots // n_experts, width)
    return lax.all_to_all(rows, EXP, split_axis=0, concat_axis=0, tiled=True).reshape(slots, width)


def everywhere(a, b, n_experts, turned):
    slots, wide = a.shape
    a = dispatched(a, n_experts)
    a0 = lax.all_gather(a, "y").reshape(NY * slots, wide)
    b = dispatched(b, n_experts)
    b0 = spread(jnp.broadcast_to(b[None], (NX,) + b.shape), "x")
    s1, t1 = ring(b0, "y", NY, 1), ring(b0, "y", NY, -1)
    a0, turned = lax.optimization_barrier((a0, turned))
    ap, am = ring(a0, "x", NX, 1), ring(a0, "x", NX, -1)
    s2, t2 = ring(s1, "y", NY, 1), ring(t1, "y", NY, -1)
    s3, t3 = ring(s2, "y", NY, 1), ring(t2, "y", NY, -1)
    s4, t4 = ring(s3[: NX // 2], "y", NY, 1), ring(t3[NX // 2 :], "y", NY, -1)
    half = NY * slots // 2
    ao0, ao1 = ring(ap[:half], "x", NX, 1), ring(am[half:], "x", NX, -1)
    return [a0, ap, ao0, ao1, am], [b0, s1, s2, s3, s4, t4, t3, t2, t1], turned


VMEM = pl.BlockSpec(memory_space=pltpu.VMEM)
SMEM = pl.BlockSpec(memory_space=pltpu.SMEM)


def body(
    conv_out,
    gate_z,
    delta_raw,
    decay_rate,
    b_proj,
    c_proj,
    skip_gain,
    out_weight,
    stream,
    norm_gain,
    expert_ids,
    gate_weights,
    w_gate,
    w_up,
):
    tokens, width = conv_out.shape
    states = decay_rate.shape[1]
    tok_rows, features = stream.shape
    n_z = lax.axis_size("z")
    n_experts = n_z * 2
    small = pltpu.CompilerParams(vmem_limit_bytes=12 * MIB)

    columns = lax.all_gather(out_weight, "y")
    place = jnp.stack([lax.axis_index("x"), lax.axis_index("y")]).astype(jnp.int32)

    rate = decay_rate.T * -LOG2E
    spans = tokens // SPAN
    b3 = b_proj.reshape(spans, SPAN, states).transpose(0, 2, 1)
    c3 = c_proj.reshape(spans, SPAN, states).transpose(0, 2, 1)
    work = tokens * width * states
    part = pl.pallas_call(
        last_kernel,
        out_shape=jax.ShapeDtypeStruct((NY, states + 8, width), jnp.float32),
        in_specs=[VMEM] * 4,
        out_specs=VMEM,
        compiler_params=small,
        cost_estimate=pl.CostEstimate(flops=4 * work, bytes_accessed=1 << 18, transcendentals=work),
    )(conv_out, delta_raw, rate, b3)
    part_shape = jax.ShapeDtypeStruct(part.shape[1:], jnp.float32)
    row_shape = jax.ShapeDtypeStruct((NX,) + part.shape[1:], jnp.float32)
    near, row = pl.pallas_call(
        row_kernel,
        out_shape=[part_shape, row_shape],
        in_specs=[SMEM, VMEM, VMEM],
        out_specs=[VMEM, VMEM],
        compiler_params=small,
        cost_estimate=pl.CostEstimate(flops=1 << 18, bytes_accessed=1 << 19, transcendentals=1 << 16),
    )(place[1:], spread(part, "y"), rate)
    rows_before = spread(row, "x")
    gated = pl.pallas_call(
        gated_kernel,
        out_shape=jax.ShapeDtypeStruct((NX, tokens, width), jnp.bfloat16),
        in_specs=[SMEM] + [VMEM] * 9,
        out_specs=VMEM,
        compiler_params=small,
        cost_estimate=pl.CostEstimate(flops=6 * work, bytes_accessed=1 << 19, transcendentals=work),
    )(place[:1], conv_out, delta_raw, gate_z, rate, b3, c3, skip_gain[None, :], near, rows_before)

    core = lax.axis_index("c").astype(jnp.int32).reshape(1)
    shape = (NX, n_z, tok_rows, features // NX)
    own, other = pl.pallas_call(
        project_kernel,
        out_shape=[jax.ShapeDtypeStruct(shape, jnp.float32), jax.ShapeDtypeStruct(shape, jnp.bfloat16)],
        in_specs=[SMEM, VMEM, VMEM],
        out_specs=[VMEM, VMEM],
        compiler_params=small,
        cost_estimate=pl.CostEstimate(
            flops=2 * tokens * width * features, bytes_accessed=width * features * 2, transcendentals=0
        ),
    )(core, spread(gated, "x"), columns)
    theirs = ring(other, "c", 2, 1)
    both = (own + theirs.astype(jnp.float32)).astype(jnp.bfloat16)
    both = both.reshape(NX * n_z, tok_rows, features // NX)
    both, wg, wu = lax.optimization_barrier((both, w_gate[0], w_up[0]))
    hidden_units = w_gate.shape[1]
    block = -(-hidden_units // TURN) * TURN
    turned = pl.pallas_call(
        turn_kernel,
        out_shape=jax.ShapeDtypeStruct((features, 2 * block), jnp.bfloat16),
        in_specs=[VMEM] * 2,
        out_specs=VMEM,
        compiler_params=small,
        cost_estimate=pl.CostEstimate(flops=1 << 24, bytes_accessed=16 * MIB, transcendentals=0),
    )(wg, wu)
    got = lax.all_to_all(both, ("x", "z"), split_axis=0, concat_axis=0, tiled=True)

    most_slots = 4 * tok_rows // n_experts
    onehot = (
        expert_ids[:, :, None] == jnp.arange(n_experts, dtype=jnp.int32)[None, None, :]
    ).astype(jnp.int32)
    flat = onehot.reshape(tok_rows * 2, n_experts)
    before = jnp.cumsum(flat, axis=0) - flat
    position = jnp.sum(before * flat, axis=1).reshape(tok_rows, 2)
    matched = (
        position[:, :, None] == jnp.arange(most_slots, dtype=jnp.int32)[None, None, :]
    ).astype(jnp.float32)
    pairs = onehot.astype(jnp.float32)[:, :, :, None] * matched[:, :, None, :]
    slots = n_experts * most_slots
    sel = jnp.sum(pairs, axis=1).reshape(tok_rows, slots).T
    gate = jnp.sum(pairs * gate_weights.astype(jnp.float32)[:, :, None, None], axis=(0, 1)).reshape(slots, 1)
    gate = jnp.pad(gate, ((0, 0), (0, PAD - 1))).astype(jnp.bfloat16)

    wide = features // 2
    a_rows, b_rows = pl.pallas_call(
        slots_kernel,
        out_shape=[
            jax.ShapeDtypeStruct((slots, wide + PAD), jnp.bfloat16),
            jax.ShapeDtypeStruct((slots, features - wide), jnp.bfloat16),
        ],
        in_specs=[VMEM] * 5,
        out_specs=[VMEM, VMEM],
        compiler_params=small,
        cost_estimate=pl.CostEstimate(flops=1 << 21, bytes_accessed=1 << 20, transcendentals=0),
    )(got, stream, norm_gain[None, :], sel, gate)
    a_parts, b_parts, turned = everywhere(a_rows, b_rows, n_experts, turned)

    total = NX * NY * slots
    result = pl.pallas_call(
        experts_kernel,
        out_shape=jax.ShapeDtypeStruct((hidden_units, total), jnp.bfloat16),
        in_specs=[SMEM] + [VMEM] * 15,
        out_specs=VMEM,
        scratch_shapes=[pltpu.VMEM((NY * slots, features - wide), jnp.bfloat16)],
        compiler_params=pltpu.CompilerParams(vmem_limit_bytes=28 * MIB),
        cost_estimate=pl.CostEstimate(
            flops=4 * hidden_units * total * features,
            bytes_accessed=total * features * 2,
            transcendentals=hidden_units * total,
        ),
    )(place, *a_parts, *b_parts, turned)
    return result[None]


def solution(mesh):
    n_z = mesh.shape["exp"] // 2
    fine = Mesh(np.asarray(mesh.devices).reshape(NX, NY, n_z, 2), ("x", "y", "z", "c"))
    in_specs = (
        P(SEQ, EXP),
        P(SEQ, EXP),
        P(SEQ, EXP),
        P(EXP, None),
        P(SEQ, None),
        P(SEQ, None),
        P(EXP),
        P(EXP, SEQ),
        P(SEQ + EXP, None),
        P(),
        P(SEQ + EXP, None),
        P(SEQ + EXP, None),
        P(EXP, SEQ, None),
        P(EXP, SEQ, None),
    )
    out_specs = P(EXP, SEQ, None)
    return jax.shard_map(body, mesh=fine, in_specs=in_specs, out_specs=out_specs, check_vma=False)
```

```python
import jax
import jax.numpy as jnp
import numpy as np
from jax import lax
from jax.experimental import pallas as pl
from jax.experimental.pallas import tpu as pltpu
from jax.sharding import Mesh
from jax.sharding import PartitionSpec as P

NX, NY = 4, 8
SEQ = ("x", "y")
EXP = ("z", "c")
LOG2E = 1.4426950408889634
SPAN = 16
PAD = 128
TURN = 256
MIB = 1024 * 1024


def softplus(v):
    return jnp.maximum(v, 0.0) + jnp.log1p(jnp.exp(-jnp.abs(v)))


def pack(ref, state, total):
    width = state.shape[1]
    lanes = ref.shape[1] - width
    ref[:, :width] = state
    rows = [total[:, k * lanes : (k + 1) * lanes] for k in range(width // lanes)]
    rows.append(jnp.zeros((state.shape[0] - len(rows), lanes), jnp.float32))
    ref[:, width:] = jnp.concatenate(rows, axis=0)


def unpack(part, width):
    lanes = part.shape[1] - width
    sums = [part[k : k + 1, width:] for k in range(width // lanes)]
    return part[:, :width], jnp.concatenate(sums, axis=1)


def last_kernel(x_ref, d_ref, rate_ref, b_ref, part_ref):
    rate = rate_ref[...]
    states, width = rate.shape

    def some(i, carry):
        state, total = carry
        rows = pl.ds(pl.multiple_of(i * SPAN, SPAN), SPAN)
        dt = softplus(d_ref[rows, :].astype(jnp.float32))
        u = dt * x_ref[rows, :].astype(jnp.float32)
        b = b_ref[i]
        for t in range(SPAN):
            step = dt[t : t + 1, :]
            state = jnp.exp2(rate * step) * state + b[:, t : t + 1] * u[t : t + 1, :]
            total = total + step
        return state, total

    start = (jnp.zeros((states, width), jnp.float32), jnp.zeros((1, width), jnp.float32))
    state, total = lax.fori_loop(0, x_ref.shape[0] // SPAN, some, start)
    for k in range(part_ref.shape[0]):
        pack(part_ref.at[k], state, total)


def row_kernel(y_ref, parts_ref, rate_ref, near_ref, row_ref):
    rate = rate_ref[...]
    states, width = rate.shape
    y = y_ref[0]
    state, total = jnp.zeros((states, width), jnp.float32), jnp.zeros((1, width), jnp.float32)
    near, near_total = state, total
    for k in range(parts_ref.shape[0]):
        own, sums = unpack(parts_ref[k], width)
        state = jnp.exp2(rate * sums) * state + own
        total = total + sums
        near = jnp.where(k + 1 == y, state, near)
        near_total = jnp.where(k + 1 == y, total, near_total)
    pack(near_ref, near, near_total)
    for k in range(row_ref.shape[0]):
        pack(row_ref.at[k], state, total)


def gated_kernel(place_ref, x_ref, d_ref, z_ref, rate_ref, b_ref, c_ref, skip_ref, near_ref, rows_ref, out_ref):
    rate = rate_ref[...]
    states, width = rate.shape
    place = lax.broadcasted_iota(jnp.int32, (SPAN, width), 0)
    start = jnp.zeros((states, width), jnp.float32)
    for k in range(rows_ref.shape[0] - 1):
        own, sums = unpack(rows_ref[k], width)
        start = jnp.where(k < place_ref[0], jnp.exp2(rate * sums) * start + own, start)
    own, sums = unpack(near_ref[...], width)
    start = jnp.exp2(rate * sums) * start + own

    def some(i, state):
        rows = pl.ds(pl.multiple_of(i * SPAN, SPAN), SPAN)
        dt = softplus(d_ref[rows, :].astype(jnp.float32))
        x = x_ref[rows, :].astype(jnp.float32)
        u = dt * x
        b, c = b_ref[i], c_ref[i]
        ssm = jnp.zeros((SPAN, width), jnp.float32)
        for t in range(SPAN):
            step = dt[t : t + 1, :]
            state = jnp.exp2(rate * step) * state + b[:, t : t + 1] * u[t : t + 1, :]
            row = jnp.sum(state * c[:, t : t + 1], axis=0, keepdims=True)
            ssm = jnp.where(place == t, row, ssm)
        z = z_ref[rows, :].astype(jnp.float32)
        gate = z / (1.0 + jnp.exp(-z))
        gated = ((ssm + skip_ref[...] * x) * gate).astype(jnp.bfloat16)
        for k in range(out_ref.shape[0]):
            out_ref[k, rows, :] = gated
        return state

    lax.fori_loop(0, x_ref.shape[0] // SPAN, some, start)


def project_kernel(core_ref, g_ref, w_ref, own_ref, other_ref):
    n_x, zs, tok, _ = own_ref.shape
    n_y, _, wide = w_ref.shape
    g = g_ref[...].reshape(n_x * zs * 2 * tok, g_ref.shape[2])
    first = core_ref[0] == 0
    for y in range(0, n_y, 2):
        w = jnp.concatenate([w_ref[y], w_ref[y + 1]], axis=1)
        p = jnp.dot(g, w, preferred_element_type=jnp.float32)
        p = p.reshape(n_x, zs, 2, tok, 2 * wide)
        a, b = p[:, :, 0], p[:, :, 1]
        at = y * wide
        own_ref[:, :, :, at : at + 2 * wide] = jnp.where(first, a, b)
        other_ref[:, :, :, at : at + 2 * wide] = jnp.where(first, b, a).astype(jnp.bfloat16)


def slots_kernel(got_ref, stream_ref, gain_ref, sel_ref, gate_ref, a_ref, b_ref):
    zs = got_ref.shape[0] // NX
    blocks = []
    for x in range(NX):
        block = got_ref[x * zs].astype(jnp.float32)
        for z in range(1, zs):
            block = block + got_ref[x * zs + z].astype(jnp.float32)
        blocks.append(block)
    resid = stream_ref[...].astype(jnp.float32) + jnp.concatenate(blocks, axis=1)
    mean = jnp.mean(resid * resid, axis=1, keepdims=True)
    normed = (resid * lax.rsqrt(mean + 1e-05) * gain_ref[...]).astype(jnp.bfloat16).astype(jnp.float32)
    sel = sel_ref[...]
    rows = sel[:, 0:1] * normed[0:1, :]
    for t in range(1, normed.shape[0]):
        rows = rows + sel[:, t : t + 1] * normed[t : t + 1, :]
    wide = a_ref.shape[1] - PAD
    a_ref[:, :wide] = rows[:, :wide].astype(jnp.bfloat16)
    a_ref[:, wide:] = gate_ref[...]
    b_ref[...] = rows[:, wide:].astype(jnp.bfloat16)


def turn_kernel(wg_ref, wu_ref, out_ref):
    units = wg_ref.shape[0]
    block = out_ref.shape[1] // 2

    def some(i, _):
        at = pl.ds(pl.multiple_of(i * TURN, TURN), TURN)
        for k, ref in enumerate((wg_ref, wu_ref)):
            w = ref[:, at].astype(jnp.float32)
            if block > units:
                w = jnp.concatenate([w, jnp.zeros((block - units, TURN), jnp.float32)], axis=0)
            out_ref[at, k * block : (k + 1) * block] = w.T.astype(jnp.bfloat16)
        return 0

    lax.fori_loop(0, wg_ref.shape[1] // TURN, some, 0)


def experts_kernel(place_ref, a0, a1, a20, a21, a3, b0, b1, b2, b3, b4, b5, b6, b7, w_ref, out_ref, b):
    my_x, my_y = place_ref[0], place_ref[1]
    units = out_ref.shape[0]
    block = w_ref.shape[1] // 2
    slots = b0.shape[1]
    wide = a0.shape[1] - PAD
    group = NY * slots
    for dx in range(NX):
        x = lax.rem(my_x - dx + NX, NX)
        for dy, ref in enumerate((b0, b1, b2, b3, b4, b5, b6, b7)):
            y = lax.rem(my_y - dy + NY, NY)
            b[pl.ds(pl.multiple_of(y * slots, slots), slots), :] = ref[x]
        if dx == 2:
            first = jnp.concatenate([a20[...], a21[...]], axis=0)
        else:
            first = (a0, a1, None, a3)[dx][...]
        p = jnp.dot(first[:, :wide], w_ref[:wide, :], preferred_element_type=jnp.float32)
        p = p + jnp.dot(b[...], w_ref[wide:, :], preferred_element_type=jnp.float32)
        gate = first[:, wide:].astype(jnp.float32)[:, 0:1]
        hidden, upward = p[:, :block], p[:, block:]
        value = hidden / (1.0 + jnp.exp(-hidden)) * upward * gate
        to = pl.ds(pl.multiple_of(x * group, group), group)
        out_ref[:, to] = value.T[:units].astype(jnp.bfloat16)


def spread(copies, axis):
    return lax.all_to_all(copies, axis, split_axis=0, concat_axis=0, tiled=True)


def ring(a, axis, size, hop):
    return lax.ppermute(a, axis, [(i, (i + hop) % size) for i in range(size)])


def dispatched(rows, n_experts):
    slots, width = rows.shape
    rows = rows.reshape(n_experts, slots // n_experts, width)
    return lax.all_to_all(rows, EXP, split_axis=0, concat_axis=0, tiled=True).reshape(slots, width)


def everywhere(a, b, n_experts):
    slots, wide = a.shape
    a = dispatched(a, n_experts)
    a0 = lax.all_gather(a, "y").reshape(NY * slots, wide)
    b = dispatched(b, n_experts)
    b0 = spread(jnp.broadcast_to(b[None], (NX,) + b.shape), "x")
    s1, t1 = ring(b0, "y", NY, 1), ring(b0, "y", NY, -1)
    ap, am = ring(a0, "x", NX, 1), ring(a0, "x", NX, -1)
    s2, t2 = ring(s1, "y", NY, 1), ring(t1, "y", NY, -1)
    s3, t3 = ring(s2, "y", NY, 1), ring(t2, "y", NY, -1)
    s4 = ring(s3, "y", NY, 1)
    half = NY * slots // 2
    ao0, ao1 = ring(ap[:half], "x", NX, 1), ring(am[half:], "x", NX, -1)
    return [a0, ap, ao0, ao1, am], [b0, s1, s2, s3, s4, t3, t2, t1]


VMEM = pl.BlockSpec(memory_space=pltpu.VMEM)
SMEM = pl.BlockSpec(memory_space=pltpu.SMEM)


def body(
    conv_out,
    gate_z,
    delta_raw,
    decay_rate,
    b_proj,
    c_proj,
    skip_gain,
    out_weight,
    stream,
    norm_gain,
    expert_ids,
    gate_weights,
    w_gate,
    w_up,
):
    tokens, width = conv_out.shape
    states = decay_rate.shape[1]
    tok_rows, features = stream.shape
    n_z = lax.axis_size("z")
    n_experts = n_z * 2
    small = pltpu.CompilerParams(vmem_limit_bytes=12 * MIB)

    columns = lax.all_gather(out_weight, "y")
    place = jnp.stack([lax.axis_index("x"), lax.axis_index("y")]).astype(jnp.int32)

    rate = decay_rate.T * -LOG2E
    spans = tokens // SPAN
    b3 = b_proj.reshape(spans, SPAN, states).transpose(0, 2, 1)
    c3 = c_proj.reshape(spans, SPAN, states).transpose(0, 2, 1)
    work = tokens * width * states
    lanes = min(PAD, width)
    part = pl.pallas_call(
        last_kernel,
        out_shape=jax.ShapeDtypeStruct((NY, states, width + lanes), jnp.float32),
        in_specs=[VMEM] * 4,
        out_specs=VMEM,
        compiler_params=pltpu.CompilerParams(vmem_limit_bytes=56 * MIB),
        cost_estimate=pl.CostEstimate(flops=4 * work, bytes_accessed=1 << 18, transcendentals=work),
    )(conv_out, delta_raw, rate, b3)
    part_shape = jax.ShapeDtypeStruct(part.shape[1:], jnp.float32)
    row_shape = jax.ShapeDtypeStruct((NX,) + part.shape[1:], jnp.float32)
    near, row = pl.pallas_call(
        row_kernel,
        out_shape=[part_shape, row_shape],
        in_specs=[SMEM, VMEM, VMEM],
        out_specs=[VMEM, VMEM],
        compiler_params=small,
        cost_estimate=pl.CostEstimate(flops=1 << 18, bytes_accessed=1 << 19, transcendentals=1 << 16),
    )(place[1:], spread(part, "y"), rate)
    rows_before = spread(row, "x")
    gated = pl.pallas_call(
        gated_kernel,
        out_shape=jax.ShapeDtypeStruct((NX, tokens, width), jnp.bfloat16),
        in_specs=[SMEM] + [VMEM] * 9,
        out_specs=VMEM,
        compiler_params=small,
        cost_estimate=pl.CostEstimate(flops=6 * work, bytes_accessed=1 << 19, transcendentals=work),
    )(place[:1], conv_out, delta_raw, gate_z, rate, b3, c3, skip_gain[None, :], near, rows_before)

    core = lax.axis_index("c").astype(jnp.int32).reshape(1)
    shape = (NX, n_z, tok_rows, features // NX)
    own, other = pl.pallas_call(
        project_kernel,
        out_shape=[jax.ShapeDtypeStruct(shape, jnp.float32), jax.ShapeDtypeStruct(shape, jnp.bfloat16)],
        in_specs=[SMEM, VMEM, VMEM],
        out_specs=[VMEM, VMEM],
        compiler_params=small,
        cost_estimate=pl.CostEstimate(
            flops=2 * tokens * width * features, bytes_accessed=width * features * 2, transcendentals=0
        ),
    )(core, spread(gated, "x"), columns)
    theirs = ring(other, "c", 2, 1)
    both = (own + theirs.astype(jnp.float32)).astype(jnp.bfloat16)
    both = both.reshape(NX * n_z, tok_rows, features // NX)
    both, wg, wu = lax.optimization_barrier((both, w_gate[0], w_up[0]))
    hidden_units = w_gate.shape[1]
    block = -(-hidden_units // TURN) * TURN
    turned = pl.pallas_call(
        turn_kernel,
        out_shape=jax.ShapeDtypeStruct((features, 2 * block), jnp.bfloat16),
        in_specs=[VMEM] * 2,
        out_specs=VMEM,
        compiler_params=small,
        cost_estimate=pl.CostEstimate(flops=1 << 24, bytes_accessed=16 * MIB, transcendentals=0),
    )(wg, wu)
    got = lax.all_to_all(both, ("x", "z"), split_axis=0, concat_axis=0, tiled=True)
    got, turned = lax.optimization_barrier((got, turned))

    most_slots = 4 * tok_rows // n_experts
    onehot = (
        expert_ids[:, :, None] == jnp.arange(n_experts, dtype=jnp.int32)[None, None, :]
    ).astype(jnp.int32)
    flat = onehot.reshape(tok_rows * 2, n_experts)
    before = jnp.cumsum(flat, axis=0) - flat
    position = jnp.sum(before * flat, axis=1).reshape(tok_rows, 2)
    matched = (
        position[:, :, None] == jnp.arange(most_slots, dtype=jnp.int32)[None, None, :]
    ).astype(jnp.float32)
    pairs = onehot.astype(jnp.float32)[:, :, :, None] * matched[:, :, None, :]
    slots = n_experts * most_slots
    sel = jnp.sum(pairs, axis=1).reshape(tok_rows, slots).T
    gate = jnp.sum(pairs * gate_weights.astype(jnp.float32)[:, :, None, None], axis=(0, 1)).reshape(slots, 1)
    gate = jnp.pad(gate, ((0, 0), (0, PAD - 1))).astype(jnp.bfloat16)

    wide = features * 17 // 32
    a_rows, b_rows = pl.pallas_call(
        slots_kernel,
        out_shape=[
            jax.ShapeDtypeStruct((slots, wide + PAD), jnp.bfloat16),
            jax.ShapeDtypeStruct((slots, features - wide), jnp.bfloat16),
        ],
        in_specs=[VMEM] * 5,
        out_specs=[VMEM, VMEM],
        compiler_params=small,
        cost_estimate=pl.CostEstimate(flops=1 << 21, bytes_accessed=1 << 20, transcendentals=0),
    )(got, stream, norm_gain[None, :], sel, gate)
    a_parts, b_parts = everywhere(a_rows, b_rows, n_experts)

    total = NX * NY * slots
    result = pl.pallas_call(
        experts_kernel,
        out_shape=jax.ShapeDtypeStruct((hidden_units, total), jnp.bfloat16),
        in_specs=[SMEM] + [VMEM] * 14,
        out_specs=VMEM,
        scratch_shapes=[pltpu.VMEM((NY * slots, features - wide), jnp.bfloat16)],
        compiler_params=pltpu.CompilerParams(vmem_limit_bytes=28 * MIB),
        cost_estimate=pl.CostEstimate(
            flops=4 * hidden_units * total * features,
            bytes_accessed=total * features * 2,
            transcendentals=hidden_units * total,
        ),
    )(place, *a_parts, *b_parts, turned)
    return result[None]


def solution(mesh):
    n_z = mesh.shape["exp"] // 2
    fine = Mesh(np.asarray(mesh.devices).reshape(NX, NY, n_z, 2), ("x", "y", "z", "c"))
    in_specs = (
        P(SEQ, EXP),
        P(SEQ, EXP),
        P(SEQ, EXP),
        P(EXP, None),
        P(SEQ, None),
        P(SEQ, None),
        P(EXP),
        P(EXP, SEQ),
        P(SEQ + EXP, None),
        P(),
        P(SEQ + EXP, None),
        P(SEQ + EXP, None),
        P(EXP, SEQ, None),
        P(EXP, SEQ, None),
    )
    out_specs = P(EXP, SEQ, None)
    return jax.shard_map(body, mesh=fine, in_specs=in_specs, out_specs=out_specs, check_vma=False)
```

```python
import jax
import jax.numpy as jnp
import numpy as np
from jax import lax
from jax.experimental import pallas as pl
from jax.experimental.pallas import tpu as pltpu
from jax.sharding import Mesh
from jax.sharding import PartitionSpec as P

NX, NY = 4, 8
SEQ = ("x", "y")
EXP = ("z", "c")
LOG2E = 1.4426950408889634
SPAN = 16
PAD = 128
TURN = 256
MIB = 1024 * 1024


def softplus(v):
    return jnp.maximum(v, 0.0) + jnp.log1p(jnp.exp(-jnp.abs(v)))


def pack(ref, state, total):
    width = state.shape[1]
    lanes = ref.shape[1] - width
    ref[:, :width] = state
    rows = [total[:, k * lanes : (k + 1) * lanes] for k in range(width // lanes)]
    rows.append(jnp.zeros((state.shape[0] - len(rows), lanes), jnp.float32))
    ref[:, width:] = jnp.concatenate(rows, axis=0)


def unpack(part, width):
    lanes = part.shape[1] - width
    sums = [part[k : k + 1, width:] for k in range(width // lanes)]
    return part[:, :width], jnp.concatenate(sums, axis=1)


def columns(ref, i):
    tokens = ref.shape[1]
    return pltpu.roll(ref[...], lax.rem(tokens - i * SPAN, tokens), 1)


def last_kernel(x_ref, d_ref, rate_ref, b_ref, part_ref):
    rate = rate_ref[...] * -LOG2E
    states, width = rate.shape

    def some(i, carry):
        state, total = carry
        rows = pl.ds(pl.multiple_of(i * SPAN, SPAN), SPAN)
        dt = softplus(d_ref[rows, :].astype(jnp.float32))
        u = dt * x_ref[rows, :].astype(jnp.float32)
        b = columns(b_ref, i)
        for t in range(SPAN):
            step = dt[t : t + 1, :]
            state = jnp.exp2(rate * step) * state + b[:, t : t + 1] * u[t : t + 1, :]
            total = total + step
        return state, total

    start = (jnp.zeros((states, width), jnp.float32), jnp.zeros((1, width), jnp.float32))
    state, total = lax.fori_loop(0, x_ref.shape[0] // SPAN, some, start)
    for k in range(part_ref.shape[0]):
        pack(part_ref.at[k], state, total)


def row_kernel(y_ref, parts_ref, rate_ref, near_ref, row_ref):
    rate = rate_ref[...] * -LOG2E
    states, width = rate.shape
    y = y_ref[0]
    state, total = jnp.zeros((states, width), jnp.float32), jnp.zeros((1, width), jnp.float32)
    near, near_total = state, total
    for k in range(parts_ref.shape[0]):
        own, sums = unpack(parts_ref[k], width)
        state = jnp.exp2(rate * sums) * state + own
        total = total + sums
        near = jnp.where(k + 1 == y, state, near)
        near_total = jnp.where(k + 1 == y, total, near_total)
    pack(near_ref, near, near_total)
    for k in range(row_ref.shape[0]):
        pack(row_ref.at[k], state, total)


def gated_kernel(place_ref, x_ref, d_ref, z_ref, rate_ref, b_ref, c_ref, skip_ref, near_ref, rows_ref, out_ref):
    rate = rate_ref[...] * -LOG2E
    states, width = rate.shape
    place = lax.broadcasted_iota(jnp.int32, (SPAN, width), 0)
    start = jnp.zeros((states, width), jnp.float32)
    for k in range(rows_ref.shape[0] - 1):
        own, sums = unpack(rows_ref[k], width)
        start = jnp.where(k < place_ref[0], jnp.exp2(rate * sums) * start + own, start)
    own, sums = unpack(near_ref[...], width)
    start = jnp.exp2(rate * sums) * start + own

    def some(i, state):
        rows = pl.ds(pl.multiple_of(i * SPAN, SPAN), SPAN)
        dt = softplus(d_ref[rows, :].astype(jnp.float32))
        x = x_ref[rows, :].astype(jnp.float32)
        u = dt * x
        b, c = columns(b_ref, i), columns(c_ref, i)
        ssm = jnp.zeros((SPAN, width), jnp.float32)
        for t in range(SPAN):
            step = dt[t : t + 1, :]
            state = jnp.exp2(rate * step) * state + b[:, t : t + 1] * u[t : t + 1, :]
            row = jnp.sum(state * c[:, t : t + 1], axis=0, keepdims=True)
            ssm = jnp.where(place == t, row, ssm)
        z = z_ref[rows, :].astype(jnp.float32)
        gate = z / (1.0 + jnp.exp(-z))
        gated = ((ssm + skip_ref[...] * x) * gate).astype(jnp.bfloat16)
        for k in range(out_ref.shape[0]):
            out_ref[k, rows, :] = gated
        return state

    lax.fori_loop(0, x_ref.shape[0] // SPAN, some, start)


def project_kernel(core_ref, g_ref, w_ref, own_ref, other_ref):
    n_x, zs, tok, _ = own_ref.shape
    n_y, _, wide = w_ref.shape
    g = g_ref[...].reshape(n_x * zs * 2 * tok, g_ref.shape[2])
    first = core_ref[0] == 0
    for y in range(0, n_y, 2):
        w = jnp.concatenate([w_ref[y], w_ref[y + 1]], axis=1)
        p = jnp.dot(g, w, preferred_element_type=jnp.float32)
        p = p.reshape(n_x, zs, 2, tok, 2 * wide)
        a, b = p[:, :, 0], p[:, :, 1]
        at = y * wide
        own_ref[:, :, :, at : at + 2 * wide] = jnp.where(first, a, b)
        other_ref[:, :, :, at : at + 2 * wide] = jnp.where(first, b, a).astype(jnp.bfloat16)


def slots_kernel(got_ref, stream_ref, gain_ref, sel_ref, gate_ref, a_ref, b_ref):
    zs = got_ref.shape[0] // NX
    blocks = []
    for x in range(NX):
        block = got_ref[x * zs].astype(jnp.float32)
        for z in range(1, zs):
            block = block + got_ref[x * zs + z].astype(jnp.float32)
        blocks.append(block)
    resid = stream_ref[...].astype(jnp.float32) + jnp.concatenate(blocks, axis=1)
    mean = jnp.mean(resid * resid, axis=1, keepdims=True)
    normed = (resid * lax.rsqrt(mean + 1e-05) * gain_ref[...]).astype(jnp.bfloat16).astype(jnp.float32)
    sel = sel_ref[...]
    rows = sel[:, 0:1] * normed[0:1, :]
    for t in range(1, normed.shape[0]):
        rows = rows + sel[:, t : t + 1] * normed[t : t + 1, :]
    wide = a_ref.shape[1] - PAD
    a_ref[:, :wide] = rows[:, :wide].astype(jnp.bfloat16)
    a_ref[:, wide:] = gate_ref[...]
    b_ref[...] = rows[:, wide:].astype(jnp.bfloat16)


def turn_kernel(wg_ref, wu_ref, out_ref):
    units = wg_ref.shape[0]
    block = out_ref.shape[1] // 2

    def some(i, _):
        at = pl.ds(pl.multiple_of(i * TURN, TURN), TURN)
        for k, ref in enumerate((wg_ref, wu_ref)):
            w = ref[:, at].astype(jnp.float32)
            if block > units:
                w = jnp.concatenate([w, jnp.zeros((block - units, TURN), jnp.float32)], axis=0)
            out_ref[at, k * block : (k + 1) * block] = w.T.astype(jnp.bfloat16)
        return 0

    lax.fori_loop(0, wg_ref.shape[1] // TURN, some, 0)


def early_kernel(a0, a1, a3, w_ref, out_ref):
    wide = a0.shape[1] - PAD
    for k, ref in enumerate((a0, a1, a3)):
        out_ref[k] = jnp.dot(ref[:, :wide], w_ref[:wide, :], preferred_element_type=jnp.float32)


def experts_kernel(place_ref, p_ref, a0, a1, a20, a21, a3, b0, b1, b2, b3, b4, b5, b6, b7, w_ref, out_ref, b):
    my_x, my_y = place_ref[0], place_ref[1]
    units = out_ref.shape[0]
    block = w_ref.shape[1] // 2
    slots = b0.shape[1]
    wide = a0.shape[1] - PAD
    group = NY * slots
    for dx in range(NX):
        x = lax.rem(my_x - dx + NX, NX)
        for dy, ref in enumerate((b0, b1, b2, b3, b4, b5, b6, b7)):
            y = lax.rem(my_y - dy + NY, NY)
            b[pl.ds(pl.multiple_of(y * slots, slots), slots), :] = ref[x]
        p = jnp.dot(b[...], w_ref[wide:, :], preferred_element_type=jnp.float32)
        if dx == 2:
            first = jnp.concatenate([a20[...], a21[...]], axis=0)
            p = p + jnp.dot(first[:, :wide], w_ref[:wide, :], preferred_element_type=jnp.float32)
            gate = first[:, wide:]
        else:
            p = p + p_ref[min(dx, 2)]
            gate = (a0, a1, None, a3)[dx][:, wide:]
        gate = gate.astype(jnp.float32)[:, 0:1]
        hidden, upward = p[:, :block], p[:, block:]
        value = hidden / (1.0 + jnp.exp(-hidden)) * upward * gate
        to = pl.ds(pl.multiple_of(x * group, group), group)
        out_ref[:, to] = value.T[:units].astype(jnp.bfloat16)


def spread(copies, axis):
    return lax.all_to_all(copies, axis, split_axis=0, concat_axis=0, tiled=True)


def ring(a, axis, size, hop):
    return lax.ppermute(a, axis, [(i, (i + hop) % size) for i in range(size)])


def dispatched(rows, n_experts):
    slots, width = rows.shape
    rows = rows.reshape(n_experts, slots // n_experts, width)
    return lax.all_to_all(rows, EXP, split_axis=0, concat_axis=0, tiled=True).reshape(slots, width)


def everywhere(a, b, n_experts):
    slots, wide = a.shape
    a = dispatched(a, n_experts)
    a0 = lax.all_gather(a, "y").reshape(NY * slots, wide)
    b = dispatched(b, n_experts)
    b0 = spread(jnp.broadcast_to(b[None], (NX,) + b.shape), "x")
    s1, t1 = ring(b0, "y", NY, 1), ring(b0, "y", NY, -1)
    ap, am = ring(a0, "x", NX, 1), ring(a0, "x", NX, -1)
    s2, t2 = ring(s1, "y", NY, 1), ring(t1, "y", NY, -1)
    s3, t3 = ring(s2, "y", NY, 1), ring(t2, "y", NY, -1)
    s4 = ring(s3, "y", NY, 1)
    half = NY * slots // 2
    ao0, ao1 = ring(ap[:half], "x", NX, 1), ring(am[half:], "x", NX, -1)
    return [a0, ap, ao0, ao1, am], [b0, s1, s2, s3, s4, t3, t2, t1]


VMEM = pl.BlockSpec(memory_space=pltpu.VMEM)
SMEM = pl.BlockSpec(memory_space=pltpu.SMEM)


def body(
    conv_out,
    gate_z,
    delta_raw,
    decay_rate,
    b_proj,
    c_proj,
    skip_gain,
    out_weight,
    stream,
    norm_gain,
    expert_ids,
    gate_weights,
    w_gate,
    w_up,
):
    tokens, width = conv_out.shape
    states = decay_rate.shape[1]
    tok_rows, features = stream.shape
    n_z = lax.axis_size("z")
    n_experts = n_z * 2
    small = pltpu.CompilerParams(vmem_limit_bytes=12 * MIB)

    gathered = lax.all_gather(out_weight, "y")
    place = jnp.stack([lax.axis_index("x"), lax.axis_index("y")]).astype(jnp.int32)

    rate, b_t, c_t = decay_rate.T, b_proj.T, c_proj.T
    work = tokens * width * states
    lanes = min(PAD, width)
    part = pl.pallas_call(
        last_kernel,
        out_shape=jax.ShapeDtypeStruct((NY, states, width + lanes), jnp.float32),
        in_specs=[VMEM] * 4,
        out_specs=VMEM,
        compiler_params=pltpu.CompilerParams(vmem_limit_bytes=56 * MIB),
        cost_estimate=pl.CostEstimate(flops=4 * work, bytes_accessed=1 << 18, transcendentals=work),
    )(conv_out, delta_raw, rate, b_t)
    part_shape = jax.ShapeDtypeStruct(part.shape[1:], jnp.float32)
    row_shape = jax.ShapeDtypeStruct((NX,) + part.shape[1:], jnp.float32)
    near, row = pl.pallas_call(
        row_kernel,
        out_shape=[part_shape, row_shape],
        in_specs=[SMEM, VMEM, VMEM],
        out_specs=[VMEM, VMEM],
        compiler_params=small,
        cost_estimate=pl.CostEstimate(flops=1 << 18, bytes_accessed=1 << 19, transcendentals=1 << 16),
    )(place[1:], spread(part, "y"), rate)
    rows_before = spread(row, "x")
    gated = pl.pallas_call(
        gated_kernel,
        out_shape=jax.ShapeDtypeStruct((NX, tokens, width), jnp.bfloat16),
        in_specs=[SMEM] + [VMEM] * 9,
        out_specs=VMEM,
        compiler_params=small,
        cost_estimate=pl.CostEstimate(flops=6 * work, bytes_accessed=1 << 19, transcendentals=work),
    )(place[:1], conv_out, delta_raw, gate_z, rate, b_t, c_t, skip_gain[None, :], near, rows_before)

    core = lax.axis_index("c").astype(jnp.int32).reshape(1)
    shape = (NX, n_z, tok_rows, features // NX)
    own, other = pl.pallas_call(
        project_kernel,
        out_shape=[jax.ShapeDtypeStruct(shape, jnp.float32), jax.ShapeDtypeStruct(shape, jnp.bfloat16)],
        in_specs=[SMEM, VMEM, VMEM],
        out_specs=[VMEM, VMEM],
        compiler_params=small,
        cost_estimate=pl.CostEstimate(
            flops=2 * tokens * width * features, bytes_accessed=width * features * 2, transcendentals=0
        ),
    )(core, spread(gated, "x"), gathered)
    theirs = ring(other, "c", 2, 1)
    both = (own + theirs.astype(jnp.float32)).astype(jnp.bfloat16)
    both = both.reshape(NX * n_z, tok_rows, features // NX)
    both, wg, wu = lax.optimization_barrier((both, w_gate[0], w_up[0]))
    hidden_units = w_gate.shape[1]
    block = -(-hidden_units // TURN) * TURN
    turned = pl.pallas_call(
        turn_kernel,
        out_shape=jax.ShapeDtypeStruct((features, 2 * block), jnp.bfloat16),
        in_specs=[VMEM] * 2,
        out_specs=VMEM,
        compiler_params=small,
        cost_estimate=pl.CostEstimate(flops=1 << 24, bytes_accessed=16 * MIB, transcendentals=0),
    )(wg, wu)
    got = lax.all_to_all(both, ("x", "z"), split_axis=0, concat_axis=0, tiled=True)
    got, turned = lax.optimization_barrier((got, turned))

    most_slots = 4 * tok_rows // n_experts
    onehot = (
        expert_ids[:, :, None] == jnp.arange(n_experts, dtype=jnp.int32)[None, None, :]
    ).astype(jnp.int32)
    flat = onehot.reshape(tok_rows * 2, n_experts)
    before = jnp.cumsum(flat, axis=0) - flat
    position = jnp.sum(before * flat, axis=1).reshape(tok_rows, 2)
    matched = (
        position[:, :, None] == jnp.arange(most_slots, dtype=jnp.int32)[None, None, :]
    ).astype(jnp.float32)
    pairs = onehot.astype(jnp.float32)[:, :, :, None] * matched[:, :, None, :]
    slots = n_experts * most_slots
    sel = jnp.sum(pairs, axis=1).reshape(tok_rows, slots).T
    gate = jnp.sum(pairs * gate_weights.astype(jnp.float32)[:, :, None, None], axis=(0, 1)).reshape(slots, 1)
    gate = jnp.pad(gate, ((0, 0), (0, PAD - 1))).astype(jnp.bfloat16)

    wide = features * 17 // 32
    a_rows, b_rows = pl.pallas_call(
        slots_kernel,
        out_shape=[
            jax.ShapeDtypeStruct((slots, wide + PAD), jnp.bfloat16),
            jax.ShapeDtypeStruct((slots, features - wide), jnp.bfloat16),
        ],
        in_specs=[VMEM] * 5,
        out_specs=[VMEM, VMEM],
        compiler_params=small,
        cost_estimate=pl.CostEstimate(flops=1 << 21, bytes_accessed=1 << 20, transcendentals=0),
    )(got, stream, norm_gain[None, :], sel, gate)
    a_parts, b_parts = everywhere(a_rows, b_rows, n_experts)

    total = NX * NY * slots
    a0, a1, _, _, a3 = a_parts
    early = pl.pallas_call(
        early_kernel,
        out_shape=jax.ShapeDtypeStruct((3, NY * slots, 2 * block), jnp.float32),
        in_specs=[VMEM] * 4,
        out_specs=VMEM,
        compiler_params=pltpu.CompilerParams(vmem_limit_bytes=20 * MIB),
        cost_estimate=pl.CostEstimate(
            flops=4 * block * 3 * NY * slots * wide, bytes_accessed=8 * MIB, transcendentals=0
        ),
    )(a0, a1, a3, turned)
    result = pl.pallas_call(
        experts_kernel,
        out_shape=jax.ShapeDtypeStruct((hidden_units, total), jnp.bfloat16),
        in_specs=[SMEM] + [VMEM] * 15,
        out_specs=VMEM,
        scratch_shapes=[pltpu.VMEM((NY * slots, features - wide), jnp.bfloat16)],
        compiler_params=pltpu.CompilerParams(vmem_limit_bytes=28 * MIB),
        cost_estimate=pl.CostEstimate(
            flops=4 * hidden_units * total * features,
            bytes_accessed=total * features * 2,
            transcendentals=hidden_units * total,
        ),
    )(place, early, *a_parts, *b_parts, turned)
    return result[None]


def solution(mesh):
    n_z = mesh.shape["exp"] // 2
    fine = Mesh(np.asarray(mesh.devices).reshape(NX, NY, n_z, 2), ("x", "y", "z", "c"))
    in_specs = (
        P(SEQ, EXP),
        P(SEQ, EXP),
        P(SEQ, EXP),
        P(EXP, None),
        P(SEQ, None),
        P(SEQ, None),
        P(EXP),
        P(EXP, SEQ),
        P(SEQ + EXP, None),
        P(),
        P(SEQ + EXP, None),
        P(SEQ + EXP, None),
        P(EXP, SEQ, None),
        P(EXP, SEQ, None),
    )
    out_specs = P(EXP, SEQ, None)
    return jax.shard_map(body, mesh=fine, in_specs=in_specs, out_specs=out_specs, check_vma=False)
```

```python
import jax
import jax.numpy as jnp
import numpy as np
from jax import lax
from jax.experimental import pallas as pl
from jax.experimental.pallas import tpu as pltpu
from jax.sharding import Mesh
from jax.sharding import PartitionSpec as P

NX, NY = 4, 8
SEQ = ("x", "y")
EXP = ("z", "c")
LOG2E = 1.4426950408889634
SPAN = 16
PAD = 128
TURN = 256
MIB = 1024 * 1024


def softplus(v):
    return jnp.maximum(v, 0.0) + jnp.log1p(jnp.exp(-jnp.abs(v)))


def pack(ref, state, total):
    width = state.shape[1]
    lanes = ref.shape[1] - width
    ref[:, :width] = state
    rows = [total[:, k * lanes : (k + 1) * lanes] for k in range(width // lanes)]
    rows.append(jnp.zeros((state.shape[0] - len(rows), lanes), jnp.float32))
    ref[:, width:] = jnp.concatenate(rows, axis=0)


def unpack(part, width):
    lanes = part.shape[1] - width
    sums = [part[k : k + 1, width:] for k in range(width // lanes)]
    return part[:, :width], jnp.concatenate(sums, axis=1)


def columns(ref, i):
    tokens = ref.shape[1]
    return pltpu.roll(ref[...], lax.rem(tokens - i * SPAN, tokens), 1)


def last_kernel(x_ref, d_ref, rate_ref, b_ref, part_ref):
    rate = rate_ref[...] * -LOG2E
    states, width = rate.shape

    def some(i, carry):
        state, total = carry
        rows = pl.ds(pl.multiple_of(i * SPAN, SPAN), SPAN)
        dt = softplus(d_ref[rows, :].astype(jnp.float32))
        u = dt * x_ref[rows, :].astype(jnp.float32)
        b = columns(b_ref, i)
        for t in range(SPAN):
            step = dt[t : t + 1, :]
            state = jnp.exp2(rate * step) * state + b[:, t : t + 1] * u[t : t + 1, :]
            total = total + step
        return state, total

    start = (jnp.zeros((states, width), jnp.float32), jnp.zeros((1, width), jnp.float32))
    state, total = lax.fori_loop(0, x_ref.shape[0] // SPAN, some, start)
    for k in range(part_ref.shape[0]):
        pack(part_ref.at[k], state, total)


def row_kernel(y_ref, parts_ref, rate_ref, near_ref, row_ref):
    rate = rate_ref[...] * -LOG2E
    states, width = rate.shape
    y = y_ref[0]
    state, total = jnp.zeros((states, width), jnp.float32), jnp.zeros((1, width), jnp.float32)
    near, near_total = state, total
    for k in range(parts_ref.shape[0]):
        own, sums = unpack(parts_ref[k], width)
        state = jnp.exp2(rate * sums) * state + own
        total = total + sums
        near = jnp.where(k + 1 == y, state, near)
        near_total = jnp.where(k + 1 == y, total, near_total)
    pack(near_ref, near, near_total)
    for k in range(row_ref.shape[0]):
        pack(row_ref.at[k], state, total)


def gated_kernel(place_ref, x_ref, d_ref, z_ref, rate_ref, b_ref, c_ref, skip_ref, near_ref, rows_ref, out_ref):
    rate = rate_ref[...] * -LOG2E
    states, width = rate.shape
    place = lax.broadcasted_iota(jnp.int32, (SPAN, width), 0)
    start = jnp.zeros((states, width), jnp.float32)
    for k in range(rows_ref.shape[0] - 1):
        own, sums = unpack(rows_ref[k], width)
        start = jnp.where(k < place_ref[0], jnp.exp2(rate * sums) * start + own, start)
    own, sums = unpack(near_ref[...], width)
    start = jnp.exp2(rate * sums) * start + own

    def some(i, state):
        rows = pl.ds(pl.multiple_of(i * SPAN, SPAN), SPAN)
        dt = softplus(d_ref[rows, :].astype(jnp.float32))
        x = x_ref[rows, :].astype(jnp.float32)
        u = dt * x
        b, c = columns(b_ref, i), columns(c_ref, i)
        ssm = jnp.zeros((SPAN, width), jnp.float32)
        for t in range(SPAN):
            step = dt[t : t + 1, :]
            state = jnp.exp2(rate * step) * state + b[:, t : t + 1] * u[t : t + 1, :]
            row = jnp.sum(state * c[:, t : t + 1], axis=0, keepdims=True)
            ssm = jnp.where(place == t, row, ssm)
        z = z_ref[rows, :].astype(jnp.float32)
        gate = z / (1.0 + jnp.exp(-z))
        gated = ((ssm + skip_ref[...] * x) * gate).astype(jnp.bfloat16)
        for k in range(out_ref.shape[0]):
            out_ref[k, rows, :] = gated
        return state

    lax.fori_loop(0, x_ref.shape[0] // SPAN, some, start)


def project_kernel(core_ref, g_ref, w_ref, own_ref, other_ref):
    n_x, zs, tok, _ = own_ref.shape
    n_y, _, wide = w_ref.shape
    g = g_ref[...].reshape(n_x * zs * 2 * tok, g_ref.shape[2])
    first = core_ref[0] == 0
    for y in range(0, n_y, 2):
        w = jnp.concatenate([w_ref[y], w_ref[y + 1]], axis=1)
        p = jnp.dot(g, w, preferred_element_type=jnp.float32)
        p = p.reshape(n_x, zs, 2, tok, 2 * wide)
        a, b = p[:, :, 0], p[:, :, 1]
        at = y * wide
        own_ref[:, :, :, at : at + 2 * wide] = jnp.where(first, a, b)
        other_ref[:, :, :, at : at + 2 * wide] = jnp.where(first, b, a).astype(jnp.bfloat16)


def slots_kernel(got_ref, stream_ref, gain_ref, sel_ref, gate_ref, a_ref, b_ref):
    zs = got_ref.shape[0] // NX
    blocks = []
    for x in range(NX):
        block = got_ref[x * zs].astype(jnp.float32)
        for z in range(1, zs):
            block = block + got_ref[x * zs + z].astype(jnp.float32)
        blocks.append(block)
    resid = stream_ref[...].astype(jnp.float32) + jnp.concatenate(blocks, axis=1)
    mean = jnp.mean(resid * resid, axis=1, keepdims=True)
    normed = (resid * lax.rsqrt(mean + 1e-05) * gain_ref[...]).astype(jnp.bfloat16).astype(jnp.float32)
    sel = sel_ref[...]
    rows = sel[:, 0:1] * normed[0:1, :]
    for t in range(1, normed.shape[0]):
        rows = rows + sel[:, t : t + 1] * normed[t : t + 1, :]
    wide = a_ref.shape[1] - PAD
    a_ref[:, :wide] = rows[:, :wide].astype(jnp.bfloat16)
    a_ref[:, wide:] = gate_ref[...]
    b_ref[...] = rows[:, wide:].astype(jnp.bfloat16)


def turn_kernel(wg_ref, wu_ref, out_ref):
    units = wg_ref.shape[0]
    block = out_ref.shape[1] // 2

    def some(i, _):
        at = pl.ds(pl.multiple_of(i * TURN, TURN), TURN)
        for k, ref in enumerate((wg_ref, wu_ref)):
            w = ref[:, at].astype(jnp.float32)
            if block > units:
                w = jnp.concatenate([w, jnp.zeros((block - units, TURN), jnp.float32)], axis=0)
            out_ref[at, k * block : (k + 1) * block] = w.T.astype(jnp.bfloat16)
        return 0

    lax.fori_loop(0, wg_ref.shape[1] // TURN, some, 0)


def block_rows(y, dy, slots):
    return pl.ds(pl.multiple_of(lax.rem(y - dy + NY, NY) * slots, slots), slots)


def early_kernel(place_ref, a0, a1, a3, b0, b1, b2, b6, b7, w_ref, out_ref, b):
    my_x, my_y = place_ref[0], place_ref[1]
    wide = a0.shape[1] - PAD
    slots = b0.shape[1]
    for dx in range(NX):
        x = lax.rem(my_x - dx + NX, NX)
        if dx == 2:
            out_ref[dx] = jnp.zeros(out_ref.shape[1:], jnp.float32)
        else:
            a = (a0, a1, None, a3)[dx]
            out_ref[dx] = jnp.dot(a[:, :wide], w_ref[:wide, :], preferred_element_type=jnp.float32)
        for k, ref in enumerate((b0, b1, b2, b6, b7)):
            b[k * slots : (k + 1) * slots, :] = ref[x]
        p = jnp.dot(b[...], w_ref[wide:, :], preferred_element_type=jnp.float32)
        for k, dy in enumerate((0, 1, 2, 6, 7)):
            out_ref[dx, block_rows(my_y, dy, slots), :] += p[k * slots : (k + 1) * slots]


def experts_kernel(place_ref, p_ref, a0, a1, a20, a21, a3, b3, b4, b5, w_ref, out_ref, b, sums):
    my_x, my_y = place_ref[0], place_ref[1]
    units = out_ref.shape[0]
    block = w_ref.shape[1] // 2
    slots = b3.shape[1]
    wide = a0.shape[1] - PAD
    group = NY * slots
    for dx in range(NX):
        x = lax.rem(my_x - dx + NX, NX)
        for k, ref in enumerate((b3, b4, b5)):
            b[k * slots : (k + 1) * slots, :] = ref[x]
        p = jnp.dot(b[...], w_ref[wide:, :], preferred_element_type=jnp.float32)
        if dx == 2:
            first = jnp.concatenate([a20[...], a21[...]], axis=0)
            early = jnp.dot(first[:, :wide], w_ref[:wide, :], preferred_element_type=jnp.float32)
            sums[...] = p_ref[dx] + early
            gate = first[:, wide:]
        else:
            sums[...] = p_ref[dx]
            gate = (a0, a1, None, a3)[dx][:, wide:]
        for k, dy in enumerate((3, 4, 5)):
            sums[block_rows(my_y, dy, slots), :] += p[k * slots : (k + 1) * slots]
        gate = gate.astype(jnp.float32)[:, 0:1]
        hidden, upward = sums[:, :block], sums[:, block:]
        value = hidden / (1.0 + jnp.exp(-hidden)) * upward * gate
        to = pl.ds(pl.multiple_of(x * group, group), group)
        out_ref[:, to] = value.T[:units].astype(jnp.bfloat16)


def spread(copies, axis):
    return lax.all_to_all(copies, axis, split_axis=0, concat_axis=0, tiled=True)


def ring(a, axis, size, hop):
    return lax.ppermute(a, axis, [(i, (i + hop) % size) for i in range(size)])


def dispatched(rows, n_experts):
    slots, width = rows.shape
    rows = rows.reshape(n_experts, slots // n_experts, width)
    return lax.all_to_all(rows, EXP, split_axis=0, concat_axis=0, tiled=True).reshape(slots, width)


def everywhere(a, b, n_experts):
    slots, wide = a.shape
    a = dispatched(a, n_experts)
    a0 = lax.all_gather(a, "y").reshape(NY * slots, wide)
    b = dispatched(b, n_experts)
    b0 = spread(jnp.broadcast_to(b[None], (NX,) + b.shape), "x")
    s1, t1 = ring(b0, "y", NY, 1), ring(b0, "y", NY, -1)
    ap, am = ring(a0, "x", NX, 1), ring(a0, "x", NX, -1)
    s2, t2 = ring(s1, "y", NY, 1), ring(t1, "y", NY, -1)
    s3, t3 = ring(s2, "y", NY, 1), ring(t2, "y", NY, -1)
    s4 = ring(s3, "y", NY, 1)
    half = NY * slots // 2
    ao0, ao1 = ring(ap[:half], "x", NX, 1), ring(am[half:], "x", NX, -1)
    return [a0, ap, ao0, ao1, am], [b0, s1, s2, s3, s4, t3, t2, t1]


VMEM = pl.BlockSpec(memory_space=pltpu.VMEM)
SMEM = pl.BlockSpec(memory_space=pltpu.SMEM)


def body(
    conv_out,
    gate_z,
    delta_raw,
    decay_rate,
    b_proj,
    c_proj,
    skip_gain,
    out_weight,
    stream,
    norm_gain,
    expert_ids,
    gate_weights,
    w_gate,
    w_up,
):
    tokens, width = conv_out.shape
    states = decay_rate.shape[1]
    tok_rows, features = stream.shape
    n_z = lax.axis_size("z")
    n_experts = n_z * 2
    small = pltpu.CompilerParams(vmem_limit_bytes=12 * MIB)

    gathered = lax.all_gather(out_weight, "y")
    place = jnp.stack([lax.axis_index("x"), lax.axis_index("y")]).astype(jnp.int32)

    rate, b_t, c_t = decay_rate.T, b_proj.T, c_proj.T
    work = tokens * width * states
    lanes = min(PAD, width)
    part = pl.pallas_call(
        last_kernel,
        out_shape=jax.ShapeDtypeStruct((NY, states, width + lanes), jnp.float32),
        in_specs=[VMEM] * 4,
        out_specs=VMEM,
        compiler_params=pltpu.CompilerParams(vmem_limit_bytes=56 * MIB),
        cost_estimate=pl.CostEstimate(flops=4 * work, bytes_accessed=1 << 18, transcendentals=work),
    )(conv_out, delta_raw, rate, b_t)
    part_shape = jax.ShapeDtypeStruct(part.shape[1:], jnp.float32)
    row_shape = jax.ShapeDtypeStruct((NX,) + part.shape[1:], jnp.float32)
    near, row = pl.pallas_call(
        row_kernel,
        out_shape=[part_shape, row_shape],
        in_specs=[SMEM, VMEM, VMEM],
        out_specs=[VMEM, VMEM],
        compiler_params=small,
        cost_estimate=pl.CostEstimate(flops=1 << 18, bytes_accessed=1 << 19, transcendentals=1 << 16),
    )(place[1:], spread(part, "y"), rate)
    rows_before = spread(row, "x")
    gated = pl.pallas_call(
        gated_kernel,
        out_shape=jax.ShapeDtypeStruct((NX, tokens, width), jnp.bfloat16),
        in_specs=[SMEM] + [VMEM] * 9,
        out_specs=VMEM,
        compiler_params=small,
        cost_estimate=pl.CostEstimate(flops=6 * work, bytes_accessed=1 << 19, transcendentals=work),
    )(place[:1], conv_out, delta_raw, gate_z, rate, b_t, c_t, skip_gain[None, :], near, rows_before)

    core = lax.axis_index("c").astype(jnp.int32).reshape(1)
    shape = (NX, n_z, tok_rows, features // NX)
    own, other = pl.pallas_call(
        project_kernel,
        out_shape=[jax.ShapeDtypeStruct(shape, jnp.float32), jax.ShapeDtypeStruct(shape, jnp.bfloat16)],
        in_specs=[SMEM, VMEM, VMEM],
        out_specs=[VMEM, VMEM],
        compiler_params=small,
        cost_estimate=pl.CostEstimate(
            flops=2 * tokens * width * features, bytes_accessed=width * features * 2, transcendentals=0
        ),
    )(core, spread(gated, "x"), gathered)
    theirs = ring(other, "c", 2, 1)
    both = (own + theirs.astype(jnp.float32)).astype(jnp.bfloat16)
    both = both.reshape(NX * n_z, tok_rows, features // NX)
    both, wg, wu = lax.optimization_barrier((both, w_gate[0], w_up[0]))
    hidden_units = w_gate.shape[1]
    block = -(-hidden_units // TURN) * TURN
    turned = pl.pallas_call(
        turn_kernel,
        out_shape=jax.ShapeDtypeStruct((features, 2 * block), jnp.bfloat16),
        in_specs=[VMEM] * 2,
        out_specs=VMEM,
        compiler_params=small,
        cost_estimate=pl.CostEstimate(flops=1 << 24, bytes_accessed=16 * MIB, transcendentals=0),
    )(wg, wu)
    got = lax.all_to_all(both, ("x", "z"), split_axis=0, concat_axis=0, tiled=True)
    got, turned = lax.optimization_barrier((got, turned))

    most_slots = 4 * tok_rows // n_experts
    onehot = (
        expert_ids[:, :, None] == jnp.arange(n_experts, dtype=jnp.int32)[None, None, :]
    ).astype(jnp.int32)
    flat = onehot.reshape(tok_rows * 2, n_experts)
    before = jnp.cumsum(flat, axis=0) - flat
    position = jnp.sum(before * flat, axis=1).reshape(tok_rows, 2)
    matched = (
        position[:, :, None] == jnp.arange(most_slots, dtype=jnp.int32)[None, None, :]
    ).astype(jnp.float32)
    pairs = onehot.astype(jnp.float32)[:, :, :, None] * matched[:, :, None, :]
    slots = n_experts * most_slots
    sel = jnp.sum(pairs, axis=1).reshape(tok_rows, slots).T
    gate = jnp.sum(pairs * gate_weights.astype(jnp.float32)[:, :, None, None], axis=(0, 1)).reshape(slots, 1)
    gate = jnp.pad(gate, ((0, 0), (0, PAD - 1))).astype(jnp.bfloat16)

    wide = features * 17 // 32
    a_rows, b_rows = pl.pallas_call(
        slots_kernel,
        out_shape=[
            jax.ShapeDtypeStruct((slots, wide + PAD), jnp.bfloat16),
            jax.ShapeDtypeStruct((slots, features - wide), jnp.bfloat16),
        ],
        in_specs=[VMEM] * 5,
        out_specs=[VMEM, VMEM],
        compiler_params=small,
        cost_estimate=pl.CostEstimate(flops=1 << 21, bytes_accessed=1 << 20, transcendentals=0),
    )(got, stream, norm_gain[None, :], sel, gate)
    a_parts, b_parts = everywhere(a_rows, b_rows, n_experts)

    total = NX * NY * slots
    a0, a1, _, _, a3 = a_parts
    late = b_parts[3:-2]
    early = pl.pallas_call(
        early_kernel,
        out_shape=jax.ShapeDtypeStruct((NX, NY * slots, 2 * block), jnp.float32),
        in_specs=[SMEM] + [VMEM] * 9,
        out_specs=VMEM,
        scratch_shapes=[pltpu.VMEM((5 * slots, features - wide), jnp.bfloat16)],
        compiler_params=pltpu.CompilerParams(vmem_limit_bytes=20 * MIB),
        cost_estimate=pl.CostEstimate(
            flops=4 * block * total * features * 2 // 3, bytes_accessed=8 * MIB, transcendentals=0
        ),
    )(place, a0, a1, a3, *b_parts[:3], *b_parts[-2:], turned)
    result = pl.pallas_call(
        experts_kernel,
        out_shape=jax.ShapeDtypeStruct((hidden_units, total), jnp.bfloat16),
        in_specs=[SMEM] + [VMEM] * (7 + len(late)),
        out_specs=VMEM,
        scratch_shapes=[
            pltpu.VMEM((3 * slots, features - wide), jnp.bfloat16),
            pltpu.VMEM((NY * slots, 2 * block), jnp.float32),
        ],
        compiler_params=pltpu.CompilerParams(vmem_limit_bytes=28 * MIB),
        cost_estimate=pl.CostEstimate(
            flops=4 * block * total * features // 3,
            bytes_accessed=total * features * 2,
            transcendentals=hidden_units * total,
        ),
    )(place, early, *a_parts, *late, turned)
    return result[None]


def solution(mesh):
    n_z = mesh.shape["exp"] // 2
    fine = Mesh(np.asarray(mesh.devices).reshape(NX, NY, n_z, 2), ("x", "y", "z", "c"))
    in_specs = (
        P(SEQ, EXP),
        P(SEQ, EXP),
        P(SEQ, EXP),
        P(EXP, None),
        P(SEQ, None),
        P(SEQ, None),
        P(EXP),
        P(EXP, SEQ),
        P(SEQ + EXP, None),
        P(),
        P(SEQ + EXP, None),
        P(SEQ + EXP, None),
        P(EXP, SEQ, None),
        P(EXP, SEQ, None),
    )
    out_specs = P(EXP, SEQ, None)
    return jax.shard_map(body, mesh=fine, in_specs=in_specs, out_specs=out_specs, check_vma=False)
```

```python
import jax
import jax.numpy as jnp
import numpy as np
from jax import lax
from jax.experimental import pallas as pl
from jax.experimental.pallas import tpu as pltpu
from jax.sharding import Mesh
from jax.sharding import PartitionSpec as P

NX, NY = 4, 8
SEQ = ("x", "y")
EXP = ("z", "c")
LOG2E = 1.4426950408889634
SPAN = 16
PAD = 128
TURN = 256
MIB = 1024 * 1024


def softplus(v):
    return jnp.maximum(v, 0.0) + jnp.log1p(jnp.exp(-jnp.abs(v)))


def pack(ref, state, total):
    width = state.shape[1]
    lanes = ref.shape[1] - width
    ref[:, :width] = state
    rows = [total[:, k * lanes : (k + 1) * lanes] for k in range(width // lanes)]
    rows.append(jnp.zeros((state.shape[0] - len(rows), lanes), jnp.float32))
    ref[:, width:] = jnp.concatenate(rows, axis=0)


def unpack(part, width):
    lanes = part.shape[1] - width
    sums = [part[k : k + 1, width:] for k in range(width // lanes)]
    return part[:, :width], jnp.concatenate(sums, axis=1)


def columns(ref, i):
    tokens = ref.shape[1]
    return pltpu.roll(ref[...], lax.rem(tokens - i * SPAN, tokens), 1)


def last_kernel(x_ref, d_ref, rate_ref, b_ref, part_ref):
    rate = rate_ref[...] * -LOG2E
    states, width = rate.shape

    def some(i, carry):
        state, total = carry
        rows = pl.ds(pl.multiple_of(i * SPAN, SPAN), SPAN)
        dt = softplus(d_ref[rows, :].astype(jnp.float32))
        u = dt * x_ref[rows, :].astype(jnp.float32)
        b = columns(b_ref, i)
        for t in range(SPAN):
            step = dt[t : t + 1, :]
            state = jnp.exp2(rate * step) * state + b[:, t : t + 1] * u[t : t + 1, :]
            total = total + step
        return state, total

    start = (jnp.zeros((states, width), jnp.float32), jnp.zeros((1, width), jnp.float32))
    state, total = lax.fori_loop(0, x_ref.shape[0] // SPAN, some, start)
    for k in range(part_ref.shape[0]):
        pack(part_ref.at[k], state, total)


def row_kernel(y_ref, parts_ref, rate_ref, near_ref, row_ref):
    rate = rate_ref[...] * -LOG2E
    states, width = rate.shape
    y = y_ref[0]
    state, total = jnp.zeros((states, width), jnp.float32), jnp.zeros((1, width), jnp.float32)
    near, near_total = state, total
    for k in range(parts_ref.shape[0]):
        own, sums = unpack(parts_ref[k], width)
        state = jnp.exp2(rate * sums) * state + own
        total = total + sums
        near = jnp.where(k + 1 == y, state, near)
        near_total = jnp.where(k + 1 == y, total, near_total)
    pack(near_ref, near, near_total)
    for k in range(row_ref.shape[0]):
        pack(row_ref.at[k], state, total)


def gated_kernel(place_ref, x_ref, d_ref, z_ref, rate_ref, b_ref, c_ref, skip_ref, near_ref, rows_ref, out_ref):
    rate = rate_ref[...] * -LOG2E
    states, width = rate.shape
    place = lax.broadcasted_iota(jnp.int32, (SPAN, width), 0)
    start = jnp.zeros((states, width), jnp.float32)
    for k in range(rows_ref.shape[0] - 1):
        own, sums = unpack(rows_ref[k], width)
        start = jnp.where(k < place_ref[0], jnp.exp2(rate * sums) * start + own, start)
    own, sums = unpack(near_ref[...], width)
    start = jnp.exp2(rate * sums) * start + own

    def some(i, state):
        rows = pl.ds(pl.multiple_of(i * SPAN, SPAN), SPAN)
        dt = softplus(d_ref[rows, :].astype(jnp.float32))
        x = x_ref[rows, :].astype(jnp.float32)
        u = dt * x
        b, c = columns(b_ref, i), columns(c_ref, i)
        ssm = jnp.zeros((SPAN, width), jnp.float32)
        for t in range(SPAN):
            step = dt[t : t + 1, :]
            state = jnp.exp2(rate * step) * state + b[:, t : t + 1] * u[t : t + 1, :]
            row = jnp.sum(state * c[:, t : t + 1], axis=0, keepdims=True)
            ssm = jnp.where(place == t, row, ssm)
        z = z_ref[rows, :].astype(jnp.float32)
        gate = z / (1.0 + jnp.exp(-z))
        gated = ((ssm + skip_ref[...] * x) * gate).astype(jnp.bfloat16)
        for k in range(out_ref.shape[0]):
            out_ref[k, rows, :] = gated
        return state

    lax.fori_loop(0, x_ref.shape[0] // SPAN, some, start)


def project_kernel(core_ref, g_ref, w_ref, own_ref, other_ref):
    n_x, zs, tok, _ = own_ref.shape
    n_y, _, wide = w_ref.shape
    g = g_ref[...].reshape(n_x * zs * 2 * tok, g_ref.shape[2])
    first = core_ref[0] == 0
    for y in range(0, n_y, 2):
        w = jnp.concatenate([w_ref[y], w_ref[y + 1]], axis=1)
        p = jnp.dot(g, w, preferred_element_type=jnp.float32)
        p = p.reshape(n_x, zs, 2, tok, 2 * wide)
        a, b = p[:, :, 0], p[:, :, 1]
        at = y * wide
        own_ref[:, :, :, at : at + 2 * wide] = jnp.where(first, a, b)
        other_ref[:, :, :, at : at + 2 * wide] = jnp.where(first, b, a).astype(jnp.bfloat16)


def slots_kernel(got_ref, stream_ref, gain_ref, sel_ref, gate_ref, a_ref, b_ref):
    zs = got_ref.shape[0] // NX
    blocks = []
    for x in range(NX):
        block = got_ref[x * zs].astype(jnp.float32)
        for z in range(1, zs):
            block = block + got_ref[x * zs + z].astype(jnp.float32)
        blocks.append(block)
    resid = stream_ref[...].astype(jnp.float32) + jnp.concatenate(blocks, axis=1)
    mean = jnp.mean(resid * resid, axis=1, keepdims=True)
    normed = (resid * lax.rsqrt(mean + 1e-05) * gain_ref[...]).astype(jnp.bfloat16).astype(jnp.float32)
    sel = sel_ref[...]
    rows = sel[:, 0:1] * normed[0:1, :]
    for t in range(1, normed.shape[0]):
        rows = rows + sel[:, t : t + 1] * normed[t : t + 1, :]
    wide = a_ref.shape[1] - PAD
    a_ref[:, :wide] = rows[:, :wide].astype(jnp.bfloat16)
    a_ref[:, wide:] = gate_ref[...]
    b_ref[...] = rows[:, wide:].astype(jnp.bfloat16)


def turn_kernel(wg_ref, wu_ref, out_ref):
    units = wg_ref.shape[0]
    block = out_ref.shape[1] // 2

    def some(i, _):
        at = pl.ds(pl.multiple_of(i * TURN, TURN), TURN)
        for k, ref in enumerate((wg_ref, wu_ref)):
            w = ref[:, at].astype(jnp.float32)
            if block > units:
                w = jnp.concatenate([w, jnp.zeros((block - units, TURN), jnp.float32)], axis=0)
            out_ref[at, k * block : (k + 1) * block] = w.T.astype(jnp.bfloat16)
        return 0

    lax.fori_loop(0, wg_ref.shape[1] // TURN, some, 0)


def block_rows(y, dy, slots):
    return pl.ds(pl.multiple_of(lax.rem(y - dy + NY, NY) * slots, slots), slots)


def early_kernel(place_ref, a0, a1, a3, b0, b1, b2, b6, b7, w_ref, out_ref, b):
    my_x, my_y = place_ref[0], place_ref[1]
    wide = a0.shape[1] - PAD
    slots = b0.shape[1]
    for dx in range(NX):
        x = lax.rem(my_x - dx + NX, NX)
        if dx == 2:
            out_ref[dx] = jnp.zeros(out_ref.shape[1:], jnp.float32)
        else:
            a = (a0, a1, None, a3)[dx]
            out_ref[dx] = jnp.dot(a[:, :wide], w_ref[:wide, :], preferred_element_type=jnp.float32)
        for k, ref in enumerate((b0, b1, b2, b6, b7)):
            b[k * slots : (k + 1) * slots, :] = ref[x]
        p = jnp.dot(b[...], w_ref[wide:, :], preferred_element_type=jnp.float32)
        for k, dy in enumerate((0, 1, 2, 6, 7)):
            out_ref[dx, block_rows(my_y, dy, slots), :] += p[k * slots : (k + 1) * slots]


def experts_kernel(place_ref, p_ref, a0, a1, a20, a21, a3, b3, b4, b5, w_ref, out_ref, b, sums):
    my_x, my_y = place_ref[0], place_ref[1]
    units = out_ref.shape[0]
    block = w_ref.shape[1] // 2
    slots = b3.shape[1]
    wide = a0.shape[1] - PAD
    group = NY * slots
    for dx in range(NX):
        x = lax.rem(my_x - dx + NX, NX)
        for k, ref in enumerate((b3, b4, b5)):
            b[k * slots : (k + 1) * slots, :] = ref[x]
        p = jnp.dot(b[...], w_ref[wide:, :], preferred_element_type=jnp.float32)
        if dx == 2:
            first = jnp.concatenate([a20[...], a21[...]], axis=0)
            early = jnp.dot(first[:, :wide], w_ref[:wide, :], preferred_element_type=jnp.float32)
            sums[...] = p_ref[dx] + early
            gate = first[:, wide:]
        else:
            sums[...] = p_ref[dx]
            gate = (a0, a1, None, a3)[dx][:, wide:]
        for k, dy in enumerate((3, 4, 5)):
            sums[block_rows(my_y, dy, slots), :] += p[k * slots : (k + 1) * slots]
        gate = gate.astype(jnp.float32)[:, 0:1]
        hidden, upward = sums[:, :block], sums[:, block:]
        value = hidden / (1.0 + jnp.exp(-hidden)) * upward * gate
        to = pl.ds(pl.multiple_of(x * group, group), group)
        out_ref[:, to] = value.T[:units].astype(jnp.bfloat16)


def spread(copies, axis):
    return lax.all_to_all(copies, axis, split_axis=0, concat_axis=0, tiled=True)


def ring(a, axis, size, hop):
    return lax.ppermute(a, axis, [(i, (i + hop) % size) for i in range(size)])


def dispatched(rows, n_experts):
    slots, width = rows.shape
    rows = rows.reshape(n_experts, slots // n_experts, width)
    return lax.all_to_all(rows, EXP, split_axis=0, concat_axis=0, tiled=True).reshape(slots, width)


def everywhere(a, b, n_experts):
    slots, wide = a.shape
    a = dispatched(a, n_experts)
    a0 = lax.all_gather(a, "y").reshape(NY * slots, wide)
    b = dispatched(b, n_experts)
    b0 = spread(jnp.broadcast_to(b[None], (NX,) + b.shape), "x")
    s1, t1 = ring(b0, "y", NY, 1), ring(b0, "y", NY, -1)
    ap, am = ring(a0, "x", NX, 1), ring(a0, "x", NX, -1)
    s2, t2 = ring(s1, "y", NY, 1), ring(t1, "y", NY, -1)
    s3, t3 = ring(s2, "y", NY, 1), ring(t2, "y", NY, -1)
    s4 = ring(s3, "y", NY, 1)
    half = NY * slots // 2
    ao0, ao1 = ring(ap[:half], "x", NX, 1), ring(am[half:], "x", NX, -1)
    return [a0, ap, ao0, ao1, am], [b0, s1, s2, s3, s4, t3, t2, t1]


VMEM = pl.BlockSpec(memory_space=pltpu.VMEM)
SMEM = pl.BlockSpec(memory_space=pltpu.SMEM)


def body(
    conv_out,
    gate_z,
    delta_raw,
    decay_rate,
    b_proj,
    c_proj,
    skip_gain,
    out_weight,
    stream,
    norm_gain,
    expert_ids,
    gate_weights,
    w_gate,
    w_up,
):
    tokens, width = conv_out.shape
    states = decay_rate.shape[1]
    tok_rows, features = stream.shape
    n_z = lax.axis_size("z")
    n_experts = n_z * 2
    small = pltpu.CompilerParams(vmem_limit_bytes=12 * MIB)

    gathered = lax.all_gather(out_weight, "y")
    place = jnp.stack([lax.axis_index("x"), lax.axis_index("y")]).astype(jnp.int32)

    rate, b_t, c_t = decay_rate.T, b_proj.T, c_proj.T
    work = tokens * width * states
    lanes = min(PAD, width)
    part = pl.pallas_call(
        last_kernel,
        out_shape=jax.ShapeDtypeStruct((NY, states, width + lanes), jnp.float32),
        in_specs=[VMEM] * 4,
        out_specs=VMEM,
        compiler_params=pltpu.CompilerParams(vmem_limit_bytes=56 * MIB),
        cost_estimate=pl.CostEstimate(flops=4 * work, bytes_accessed=1 << 18, transcendentals=work),
    )(conv_out, delta_raw, rate, b_t)
    part_shape = jax.ShapeDtypeStruct(part.shape[1:], jnp.float32)
    row_shape = jax.ShapeDtypeStruct((NX,) + part.shape[1:], jnp.float32)
    near, row = pl.pallas_call(
        row_kernel,
        out_shape=[part_shape, row_shape],
        in_specs=[SMEM, VMEM, VMEM],
        out_specs=[VMEM, VMEM],
        compiler_params=small,
        cost_estimate=pl.CostEstimate(flops=1 << 18, bytes_accessed=1 << 19, transcendentals=1 << 16),
    )(place[1:], spread(part, "y"), rate)
    rows_before = spread(row, "x")
    gated = pl.pallas_call(
        gated_kernel,
        out_shape=jax.ShapeDtypeStruct((NX, tokens, width), jnp.bfloat16),
        in_specs=[SMEM] + [VMEM] * 9,
        out_specs=VMEM,
        compiler_params=small,
        cost_estimate=pl.CostEstimate(flops=6 * work, bytes_accessed=1 << 19, transcendentals=work),
    )(place[:1], conv_out, delta_raw, gate_z, rate, b_t, c_t, skip_gain[None, :], near, rows_before)

    core = lax.axis_index("c").astype(jnp.int32).reshape(1)
    shape = (NX, n_z, tok_rows, features // NX)
    own, other = pl.pallas_call(
        project_kernel,
        out_shape=[jax.ShapeDtypeStruct(shape, jnp.float32), jax.ShapeDtypeStruct(shape, jnp.bfloat16)],
        in_specs=[SMEM, VMEM, VMEM],
        out_specs=[VMEM, VMEM],
        compiler_params=small,
        cost_estimate=pl.CostEstimate(
            flops=2 * tokens * width * features, bytes_accessed=width * features * 2, transcendentals=0
        ),
    )(core, spread(gated, "x"), gathered)
    theirs = ring(other, "c", 2, 1)
    both = (own + theirs.astype(jnp.float32)).astype(jnp.bfloat16)
    both = both.reshape(NX * n_z, tok_rows, features // NX)
    both, wg, wu = lax.optimization_barrier((both, w_gate[0], w_up[0]))
    hidden_units = w_gate.shape[1]
    block = -(-hidden_units // TURN) * TURN
    turned = pl.pallas_call(
        turn_kernel,
        out_shape=jax.ShapeDtypeStruct((features, 2 * block), jnp.bfloat16),
        in_specs=[VMEM] * 2,
        out_specs=VMEM,
        compiler_params=small,
        cost_estimate=pl.CostEstimate(flops=1 << 24, bytes_accessed=16 * MIB, transcendentals=0),
    )(wg, wu)
    got = lax.all_to_all(both, ("x", "z"), split_axis=0, concat_axis=0, tiled=True)
    got, turned = lax.optimization_barrier((got, turned))

    most_slots = 4 * tok_rows // n_experts
    onehot = (
        expert_ids[:, :, None] == jnp.arange(n_experts, dtype=jnp.int32)[None, None, :]
    ).astype(jnp.int32)
    flat = onehot.reshape(tok_rows * 2, n_experts)
    before = jnp.cumsum(flat, axis=0) - flat
    position = jnp.sum(before * flat, axis=1).reshape(tok_rows, 2)
    matched = (
        position[:, :, None] == jnp.arange(most_slots, dtype=jnp.int32)[None, None, :]
    ).astype(jnp.float32)
    pairs = onehot.astype(jnp.float32)[:, :, :, None] * matched[:, :, None, :]
    slots = n_experts * most_slots
    sel = jnp.sum(pairs, axis=1).reshape(tok_rows, slots).T
    gate = jnp.sum(pairs * gate_weights.astype(jnp.float32)[:, :, None, None], axis=(0, 1)).reshape(slots, 1)
    gate = jnp.pad(gate, ((0, 0), (0, PAD - 1))).astype(jnp.bfloat16)

    wide = features * 18 // 32
    a_rows, b_rows = pl.pallas_call(
        slots_kernel,
        out_shape=[
            jax.ShapeDtypeStruct((slots, wide + PAD), jnp.bfloat16),
            jax.ShapeDtypeStruct((slots, features - wide), jnp.bfloat16),
        ],
        in_specs=[VMEM] * 5,
        out_specs=[VMEM, VMEM],
        compiler_params=small,
        cost_estimate=pl.CostEstimate(flops=1 << 21, bytes_accessed=1 << 20, transcendentals=0),
    )(got, stream, norm_gain[None, :], sel, gate)
    a_parts, b_parts = everywhere(a_rows, b_rows, n_experts)

    total = NX * NY * slots
    a0, a1, _, _, a3 = a_parts
    late = b_parts[3:-2]
    early = pl.pallas_call(
        early_kernel,
        out_shape=jax.ShapeDtypeStruct((NX, NY * slots, 2 * block), jnp.float32),
        in_specs=[SMEM] + [VMEM] * 9,
        out_specs=VMEM,
        scratch_shapes=[pltpu.VMEM((5 * slots, features - wide), jnp.bfloat16)],
        compiler_params=pltpu.CompilerParams(vmem_limit_bytes=20 * MIB),
        cost_estimate=pl.CostEstimate(
            flops=4 * block * total * features * 2 // 3, bytes_accessed=8 * MIB, transcendentals=0
        ),
    )(place, a0, a1, a3, *b_parts[:3], *b_parts[-2:], turned)
    result = pl.pallas_call(
        experts_kernel,
        out_shape=jax.ShapeDtypeStruct((hidden_units, total), jnp.bfloat16),
        in_specs=[SMEM] + [VMEM] * (7 + len(late)),
        out_specs=VMEM,
        scratch_shapes=[
            pltpu.VMEM((3 * slots, features - wide), jnp.bfloat16),
            pltpu.VMEM((NY * slots, 2 * block), jnp.float32),
        ],
        compiler_params=pltpu.CompilerParams(vmem_limit_bytes=28 * MIB),
        cost_estimate=pl.CostEstimate(
            flops=4 * block * total * features // 3,
            bytes_accessed=total * features * 2,
            transcendentals=hidden_units * total,
        ),
    )(place, early, *a_parts, *late, turned)
    return result[None]


def solution(mesh):
    n_z = mesh.shape["exp"] // 2
    fine = Mesh(np.asarray(mesh.devices).reshape(NX, NY, n_z, 2), ("x", "y", "z", "c"))
    in_specs = (
        P(SEQ, EXP),
        P(SEQ, EXP),
        P(SEQ, EXP),
        P(EXP, None),
        P(SEQ, None),
        P(SEQ, None),
        P(EXP),
        P(EXP, SEQ),
        P(SEQ + EXP, None),
        P(),
        P(SEQ + EXP, None),
        P(SEQ + EXP, None),
        P(EXP, SEQ, None),
        P(EXP, SEQ, None),
    )
    out_specs = P(EXP, SEQ, None)
    return jax.shard_map(body, mesh=fine, in_specs=in_specs, out_specs=out_specs, check_vma=False)
```
